512 devices in a mesh: seq: 64 (over y_hi, z, core), chan: 8 (over x, y_lo).
Axes of the slice: x: 4, y: 4 (y_hi: 2, y_lo: 2; y = y_hi * 2 + y_lo), z: 16, core: 2. Of those that a mesh axis runs over, the one named last changes fastest.
Arguments:
- query_gate: bfloat16 [8192, 8192], P('seq', 'chan'), may hold values from -6 to 6
- key_gate: bfloat16 [8192, 8192], P('seq', 'chan'), may hold values from -6 to 6
- value_input: bfloat16 [8192, 8192], P('seq', 'chan'), may hold values from -6 to 6
- grad_out: bfloat16 [8192, 8192], P('seq', 'chan'), may hold values from -6 to 6
- residues: float32 [8192, 16], P(('chan', 'seq')), may hold values from -1.5 to 1.5
- decay: float32 [8192, 16], P(('chan', 'seq')), as said below
Outputs:
- grad_query: bfloat16 [8192, 8192], P('seq', 'chan')
- grad_key: bfloat16 [8192, 8192], P('seq', 'chan')
- grad_value: bfloat16 [8192, 8192], P('seq', 'chan')
- grad_residues: float32 [8192, 16], P(('chan', 'seq'))
The draws below stay inside these ranges and needn't reach their ends.
Inputs may be any that keep to these rules, and one draw needn't show every extreme that they name: `decay`: positive rates, none above 0.1.
All inputs are finite; a program needn't handle non-finite values.
Results may differ from the reference program's by a relative error of at most 0.011.
Values may be sent and summed in bfloat16 or wider, within the bound.
A program may use at most 128 MiB of HBM per device.

```python
import math
import jax
import jax.numpy as jnp
from jax import lax

C = 8192
M = 16
LENGTH = 8192


def draw_decay(key, part):
    key = jax.random.fold_in(key, 7)
    pick_key, slow_key, fast_key = jax.random.split(key, 3)
    share = 0.5
    slow_mask = jax.random.uniform(pick_key, (C, M), dtype=jnp.float32) < share
    slow = jnp.exp(jax.random.uniform(slow_key, (C, M), dtype=jnp.float32, minval=math.log(0.3 / LENGTH), maxval=math.log(2.3 / LENGTH)))
    fast = jnp.exp(jax.random.uniform(fast_key, (C, M), dtype=jnp.float32, minval=math.log(0.02), maxval=math.log(0.1)))
    return jnp.where(slow_mask, slow, fast).astype(jnp.float32)


def level_of(stream_key, shape, cuts, low, top_value):
    def one(position, shards_of):
        heights = jax.random.uniform(jax.random.fold_in(jax.random.fold_in(stream_key, 6), position), (shards_of,), jnp.float32, low / len(cuts), top_value / len(cuts))
        return jnp.repeat(jnp.exp(heights), shape[position] // shards_of).reshape((-1,) + (1,) * (len(shape) - position - 1))

    loudness = one(*cuts[0])
    for cut in cuts[1:]:
        loudness = loudness * one(*cut)
    return loudness


def bell_draw(own_key, dims, spread, limit, cuts=(), kind=jnp.bfloat16):
    level = level_of(own_key, dims, cuts, -0.22, 0.18) if cuts else 1.0
    values = jax.random.normal(own_key, dims, jnp.float32) * spread * level
    return jnp.minimum(jnp.maximum(values, -limit), limit).astype(kind)


def setup_inputs(seed: int = 0) -> dict:
    splits = jax.random.split(jax.random.key(seed), 7)
    query_gate = bell_draw(splits[0], (LENGTH, C), 1.0, 6.0, ((0, 64), (1, 8)))
    key_gate = bell_draw(splits[1], (LENGTH, C), 1.0, 6.0, ((0, 64), (1, 8)))
    value_input = bell_draw(splits[2], (LENGTH, C), 1.0, 6.0, ((0, 64), (1, 8)))
    grad_out = bell_draw(splits[3], (LENGTH, C), 1.0, 6.0, ((0, 64), (1, 8)))
    residues = bell_draw(splits[4], (C, M), M ** -0.5, 1.5, ((0, 512),), jnp.float32)
    decay = draw_decay(jax.random.fold_in(splits[6], 71), 0)
    return {"query_gate": query_gate, "key_gate": key_gate, "value_input": value_input, "grad_out": grad_out, "residues": residues, "decay": decay}


def reference(query_gate, key_gate, value_input, grad_out, residues, decay):
    width = 64
    count = C // width
    span = 2 * LENGTH
    conv_input = (key_gate.astype(jnp.float32) * value_input.astype(jnp.float32)).astype(jnp.bfloat16)
    conv_grad = (grad_out.astype(jnp.float32) * query_gate.astype(jnp.float32)).astype(jnp.bfloat16)
    input_f, grad_f = lax.optimization_barrier((conv_input, conv_grad))
    input_f = input_f.astype(jnp.float32)
    grad_f = grad_f.astype(jnp.float32)
    mode_scale = jnp.sqrt(1.0 - jnp.exp(-2.0 * decay))
    gain = residues * mode_scale
    input_blocks = input_f.reshape(LENGTH, count, width).transpose(1, 2, 0)
    grad_blocks = grad_f.reshape(LENGTH, count, width).transpose(1, 2, 0)
    gain_blocks = gain.reshape(count, width, M)
    decay_blocks = decay.reshape(count, width, M)
    lag_pos = jnp.arange(LENGTH, dtype=jnp.float32)

    def one_block(items):
        block_in, block_grad, block_gain, block_decay = items
        table = jnp.exp(-block_decay[:, :, None] * lag_pos)
        taps = jnp.einsum('cm,cmd->cd', block_gain, table, precision=lax.Precision.HIGHEST)
        in_freq = jnp.fft.rfft(block_in, n=span)
        grad_freq = jnp.fft.rfft(block_grad, n=span)
        tap_freq = jnp.fft.rfft(taps, n=span)
        forward = jnp.fft.irfft(in_freq * tap_freq, n=span)[:, :LENGTH]
        backward = jnp.fft.irfft(grad_freq * jnp.conj(tap_freq), n=span)[:, :LENGTH]
        lagged = jnp.fft.irfft(grad_freq * jnp.conj(in_freq), n=span)[:, :LENGTH]
        score = jnp.einsum('cd,cmd->cm', lagged, table, precision=lax.Precision.HIGHEST)
        return (forward, backward, score)
    forward, backward, score = lax.map(one_block, (input_blocks, grad_blocks, gain_blocks, decay_blocks))
    conv_output = forward.transpose(2, 0, 1).reshape(LENGTH, C).astype(jnp.bfloat16)
    input_grad = backward.transpose(2, 0, 1).reshape(LENGTH, C).astype(jnp.bfloat16)
    grad_query = (grad_out.astype(jnp.float32) * conv_output.astype(jnp.float32)).astype(jnp.bfloat16)
    grad_key = (input_grad.astype(jnp.float32) * value_input.astype(jnp.float32)).astype(jnp.bfloat16)
    grad_value = (input_grad.astype(jnp.float32) * key_gate.astype(jnp.float32)).astype(jnp.bfloat16)
    grad_residues = mode_scale * score.reshape(C, M) * (1.0 / math.sqrt(LENGTH))
    return (grad_query, grad_key, grad_value, grad_residues)
```

```python
import functools
import math

import jax
import jax.numpy as jnp
import ml_dtypes
import numpy as np
from jax import lax
from jax.experimental import pallas as pl
from jax.experimental.pallas import tpu as pltpu
from jax.sharding import PartitionSpec as P

MESH = pl.DeviceIdType.MESH
F32 = jnp.float32
BF16 = jnp.bfloat16
SPAN = 128
NODES = 16
MODES = 16
BLOCKS = 8
CHUNKS = 64
OWN = 16
Z_FIRST, Z_STEP = 12, 1


def scan_device(block, core):
    z = (Z_FIRST + Z_STEP * (block % 4)) % 16
    return (block // 4) * 32 + z * 2 + core


def nodes():
    k = np.arange(NODES)
    half = (SPAN - 1) / 2.0
    return half + half * np.cos(np.pi * (2 * k + 1) / (2 * NODES))


def cardinal():
    t = nodes()
    lag = np.arange(SPAN, dtype=np.float64)
    out = np.ones((NODES, SPAN))
    for k in range(NODES):
        for j in range(NODES):
            if j != k:
                out[k] *= (lag - t[j]) / (t[k] - t[j])
    return out


def split(a):
    high = a.astype(ml_dtypes.bfloat16)
    low = (a - high.astype(np.float64)).astype(ml_dtypes.bfloat16)
    return np.concatenate([high, low], axis=-1)


@functools.cache
def tables():
    phi = cardinal()
    t = np.arange(SPAN)
    lag = t[:, None] - t[None, :]
    inside = lag >= 0
    low = np.where(inside[None], phi[:, np.where(inside, lag, 0)], 0.0)
    forward = low.reshape(NODES * SPAN, SPAN)
    backward = low.transpose(0, 2, 1).reshape(NODES * SPAN, SPAN)
    toeplitz = np.stack([split(forward), split(backward)])
    moments = np.stack([split(phi[:, ::-1]), split(phi)])
    spread = np.stack([split(phi.T), split(phi[:, ::-1].T)])
    return toeplitz, moments, spread


def falling(u):
    total = jnp.full_like(u, -1.0 / 5040.0)
    for c in (720.0, -120.0, 24.0, -6.0, 2.0, -1.0):
        total = total * u - 1.0 / c
    return total * u


def kernel(
    q_hbm, k_hbm, v_hbm, go_hbm, res_hbm, dec_hbm, toe_hbm, mom_hbm, spr_hbm,
    y_out, r_out, s_out,
    q_in, k_in, v_in, go_in, res_in, dec_in, toe, mom, spr,
    x2, g2, prod, inn, y_acc, r_acc,
    mom_send, inn_send, prm_send,
    mom_rcv, inn_rcv, prm_rcv, kap_rcv, ent_rcv, sco_rcv, sib_rcv,
    psi, push, ebuf, before, ent_send, kap_send, sco_send,
    in_sem, send_sem, recv_sem,
):
    me = lax.axis_index("seq")
    core = lax.rem(me, 2)
    z = lax.rem(lax.div(me, 2), 16)
    y_hi = lax.div(me, 32)
    ahead = lax.rem(z - Z_FIRST + 16, 16)
    scans = jnp.logical_and(lax.rem(ahead, Z_STEP) == 0, ahead < 4 * Z_STEP)
    block = y_hi * 4 + lax.rem(lax.div(ahead, Z_STEP), 4)
    own_block, own_part = lax.div(me, 8), lax.rem(me, 8)
    scanners = [(b, c, scan_device(b, c)) for b in range(BLOCKS) for c in range(2)]

    loads = [
        pltpu.make_async_copy(src, dst, in_sem.at[n])
        for n, (src, dst) in enumerate(
            [
                (k_hbm, k_in), (v_hbm, v_in), (go_hbm, go_in), (q_hbm, q_in),
                (mom_hbm, mom), (res_hbm, res_in), (dec_hbm, dec_in), (spr_hbm, spr), (toe_hbm, toe),
            ]
        )
    ]
    for load in loads:
        load.start()

    barrier = pltpu.get_barrier_semaphore()

    def greet(device):
        pl.semaphore_signal(barrier, inc=1, device_id={"seq": device}, device_id_type=MESH)

    @pl.when(scans)
    def _():
        def one(n, carry):
            greet(lax.rem(me + n, CHUNKS))
            return carry

        lax.fori_loop(1, CHUNKS, one, 0)

    @pl.when(jnp.logical_not(scans))
    def _():
        for _, _, device in scanners:
            greet(device)

    for n in (0, 1, 2, 3, 4):
        loads[n].wait()
    x = (k_in[...].astype(F32) * v_in[...].astype(F32)).astype(BF16)
    g = (go_in[...].astype(F32) * q_in[...].astype(F32)).astype(BF16)
    x2[:SPAN, :] = x
    x2[SPAN:, :] = x
    g2[:SPAN, :] = g
    g2[SPAN:, :] = g
    for c, ref in ((0, x2), (1, g2)):
        value = jnp.dot(mom[c], ref[...], preferred_element_type=F32).astype(BF16)
        for b in range(BLOCKS):
            mom_send[c, b] = value[:, b * SPAN : (b + 1) * SPAN]

    loads[5].wait()
    loads[6].wait()
    lane16 = lax.broadcasted_iota(jnp.int32, (OWN, SPAN), 1)
    row16 = lax.broadcasted_iota(jnp.int32, (OWN, SPAN), 0)
    for n, ref in ((0, dec_in), (1, res_in)):
        value = ref[...]
        for r in range(2):
            wide = jnp.zeros((OWN, SPAN), F32)
            for j in range(8):
                column = jnp.broadcast_to(value[:, 8 * r + j : 8 * r + j + 1], (OWN, SPAN))
                wide = jnp.where(lane16 // 16 == j, column, wide)
            wide = jnp.where(lane16 % 16 == row16, wide, 0.0)
            prm_send[2 * n + r : 2 * n + r + 1, :] = jnp.sum(wide, axis=0, keepdims=True)

    @pl.when(scans)
    def _():
        pl.semaphore_wait(barrier, CHUNKS - 1)

    @pl.when(jnp.logical_not(scans))
    def _():
        pl.semaphore_wait(barrier, 2 * BLOCKS)

    def push_to(src, dst, kind, device):
        return pltpu.make_async_remote_copy(
            src_ref=src, dst_ref=dst, send_sem=send_sem.at[kind], recv_sem=recv_sem.at[kind],
            device_id={"seq": device}, device_id_type=MESH,
        )

    def send(src, dst, kind, device):
        @pl.when(me != device)
        def _():
            push_to(src, dst, kind, device).start()

        @pl.when(me == device)
        def _():
            pltpu.make_async_copy(src, dst, recv_sem.at[kind]).start()

    def sent(src, dst, kind, device):
        @pl.when(me != device)
        def _():
            push_to(src, dst, kind, device).wait_send()

    def arrived(ref, kind):
        pltpu.make_async_copy(ref, ref, recv_sem.at[kind]).wait()

    MOM, INN, PRM, KAP, ENT, SCO, SIB = range(7)
    moment_args = [(mom_send.at[c, b], mom_rcv.at[me], MOM, device) for b, c, device in scanners]
    inner_args = [(inn_send.at[b], inn_rcv.at[me], INN, device) for b, c, device in scanners if c == 0]
    for args in moment_args:
        send(*args)
    own_scan = [
        lax.div(own_block, 4) * 32
        + lax.rem(Z_FIRST + Z_STEP * lax.rem(own_block, 4), 16) * 2
        + c
        for c in range(2)
    ]
    param_args = [(prm_send, prm_rcv.at[own_part], PRM, device) for device in own_scan]
    for args in param_args:
        send(*args)

    loads[7].wait()
    loads[8].wait()

    def local(j, carry):
        cols = pl.ds(pl.multiple_of(j * 256, 256), 256)
        prod[0, :, cols] = jnp.dot(toe[0], x2[:, cols], preferred_element_type=F32)
        prod[1, :, cols] = jnp.dot(toe[1], g2[:, cols], preferred_element_type=F32)
        grad = g2[:SPAN, cols].astype(F32)
        for k in range(NODES):
            inn[k : k + 1, cols] = jnp.sum(
                prod[0, k * SPAN : (k + 1) * SPAN, cols] * grad, axis=0, keepdims=True
            )
        return carry

    lax.fori_loop(0, 4, local, 0)
    for b in range(BLOCKS):
        inn_send[b] = inn[:, b * SPAN : (b + 1) * SPAN].astype(BF16)
    for args in inner_args:
        send(*args)

    def chunk_at(i):
        return i + core * (CHUNKS - 1 - 2 * i)

    @pl.when(scans)
    def _():
        arrived(prm_rcv, PRM)
        lane8 = lax.broadcasted_iota(jnp.int32, (8, SPAN), 1)
        row8 = lax.broadcasted_iota(jnp.int32, (8, SPAN), 0)
        halves = []
        for r in range(4):
            packed = jnp.concatenate([prm_rcv[k, r : r + 1, :] for k in range(8)], axis=0)
            skewed = pltpu.roll(packed, 0, 1, stride=16, stride_axis=0)
            out = jnp.zeros((8, SPAN), F32)
            for j in range(8):
                turned = pltpu.roll(skewed, (SPAN - 16 * j) % SPAN, 1)
                turned = jnp.where(lane8 // 16 == row8, turned, 0.0)
                out = jnp.where(row8 == j, jnp.sum(turned, axis=0, keepdims=True), out)
            halves.append(out)
        decay = jnp.concatenate(halves[:2], axis=0)
        residue = jnp.concatenate(halves[2:], axis=0)
        scale = jnp.sqrt(falling(2.0 * decay))
        gain = residue * scale
        keep = 1.0 - falling(decay)
        points = nodes()
        for k in range(NODES):
            psi[k] = jnp.exp(decay * float(-points[k]))
        where = jnp.zeros((NODES, SPAN), F32)
        rows = lax.broadcasted_iota(jnp.int32, (NODES, SPAN), 0)
        for k in range(NODES):
            where = jnp.where(rows == k, float(-points[k]), where)
        kappa = jnp.zeros((NODES, SPAN), F32)
        for m in range(MODES):
            wave = jnp.exp(where * decay[m : m + 1, :]) * gain[m : m + 1, :]
            kappa = kappa + wave
            push[m] = wave * keep[m : m + 1, :]
        kap_send[...] = kappa

        def tell(n, carry):
            send(kap_send, kap_rcv.at[block], KAP, 2 * n + core)
            return carry

        lax.fori_loop(0, CHUNKS // 2, tell, 0)

        arrived(mom_rcv, MOM)

        def expand(b, carry):
            mu = mom_rcv[b].astype(F32)
            total = psi[0] * mu[0:1, :]
            for k in range(1, NODES):
                total = total + psi[k] * mu[k : k + 1, :]
            ebuf[b] = total
            return carry

        lax.fori_loop(0, CHUNKS, expand, 0)

        @pl.when(core == 1)
        def _():
            push_to(ebuf, sib_rcv, SIB, me - 1).start()

        far = jnp.exp(decay * float(-SPAN))

        def step(i, state):
            b = chunk_at(i)
            before[b] = state
            total = push[0] * state[0:1, :]
            for m in range(1, MODES):
                total = total + push[m] * state[m : m + 1, :]
            ent_send[b] = total.astype(BF16)
            send(ent_send.at[b], ent_rcv.at[core, block], ENT, b)
            return state * far + ebuf[b]

        lax.fori_loop(0, CHUNKS, step, jnp.zeros((MODES, SPAN), F32))

        @pl.when(core == 0)
        def _():
            arrived(sib_rcv, SIB)
            arrived(inn_rcv, INN)

            def cross(b, carry):
                total, inner = carry
                return total + before[b] * sib_rcv[b], inner + inn_rcv[b].astype(F32)

            zero = jnp.zeros((MODES, SPAN), F32)
            total, inner = lax.fori_loop(0, CHUNKS, cross, (zero, zero))
            total = total * keep
            for k in range(NODES):
                total = total + psi[k] * inner[k : k + 1, :]
            sco_send[...] = total * scale * (1.0 / math.sqrt(SPAN * CHUNKS))
            for k in range(8):
                send(sco_send, sco_rcv, SCO, 8 * block + k)

    arrived(kap_rcv, KAP)

    def gather(b, carry):
        cols = pl.ds(pl.multiple_of(b * SPAN, SPAN), SPAN)
        kappa = kap_rcv[b]
        for c, acc in ((0, y_acc), (1, r_acc)):
            total = prod[c, :SPAN, cols] * kappa[0:1, :]
            for k in range(1, NODES):
                total = total + prod[c, k * SPAN : (k + 1) * SPAN, cols] * kappa[k : k + 1, :]
            acc[:, cols] = total
        return carry

    lax.fori_loop(0, BLOCKS, gather, 0)
    arrived(ent_rcv, ENT)
    for b in range(BLOCKS):
        cols = slice(b * SPAN, (b + 1) * SPAN)
        for c, acc, out in ((0, y_acc, y_out), (1, r_acc, r_out)):
            entering = ent_rcv[c, b]
            both = jnp.concatenate([entering, entering], axis=0)
            total = acc[:, cols] + jnp.dot(spr[c], both, preferred_element_type=F32)
            out[:, cols] = total.astype(BF16)

    arrived(sco_rcv, SCO)
    s_out[...] = pltpu.roll(sco_rcv[...], lax.rem(SPAN - 16 * own_part, SPAN), 1)

    for args in moment_args + inner_args + param_args:
        sent(*args)

    @pl.when(scans)
    def _():
        def told(n, carry):
            sent(kap_send, kap_rcv.at[block], KAP, 2 * n + core)
            return carry

        lax.fori_loop(0, CHUNKS // 2, told, 0)

        def stepped(b, carry):
            sent(ent_send.at[b], ent_rcv.at[core, block], ENT, b)
            return carry

        lax.fori_loop(0, CHUNKS, stepped, 0)

        @pl.when(core == 1)
        def _():
            push_to(ebuf, sib_rcv, SIB, me - 1).wait_send()

        @pl.when(core == 0)
        def _():
            for k in range(8):
                sent(sco_send, sco_rcv, SCO, 8 * block + k)


def gated(left, right):
    return (left.astype(F32) * right.astype(F32)).astype(BF16)


def body(query_gate, key_gate, value_input, grad_out, residues, decay):
    toeplitz, moments, spread = (jnp.asarray(t) for t in tables())
    tokens, channels = query_gate.shape
    vm = pltpu.VMEM
    gate = vm((tokens, channels), BF16)
    scratch = [
        gate, gate, gate, gate, vm((OWN, MODES), F32), vm((OWN, MODES), F32),
        vm(toeplitz.shape, BF16), vm(moments.shape, BF16), vm(spread.shape, BF16),
        vm((2 * tokens, channels), BF16), vm((2 * tokens, channels), BF16),
        vm((2, NODES * SPAN, channels), F32), vm((NODES, channels), F32),
        vm((tokens, channels), F32), vm((tokens, channels), F32),
        vm((2, BLOCKS, NODES, SPAN), BF16), vm((BLOCKS, NODES, SPAN), BF16), vm((4, SPAN), F32),
        vm((CHUNKS, NODES, SPAN), BF16), vm((CHUNKS, NODES, SPAN), BF16), vm((8, 4, SPAN), F32),
        vm((BLOCKS, NODES, SPAN), F32), vm((2, BLOCKS, NODES, SPAN), BF16), vm((MODES, SPAN), F32),
        vm((CHUNKS, MODES, SPAN), F32),
        vm((NODES, MODES, SPAN), F32), vm((MODES, NODES, SPAN), F32), vm((CHUNKS, MODES, SPAN), F32),
        vm((CHUNKS, MODES, SPAN), F32), vm((CHUNKS, NODES, SPAN), BF16), vm((NODES, SPAN), F32),
        vm((MODES, SPAN), F32),
        pltpu.SemaphoreType.DMA((9,)), pltpu.SemaphoreType.DMA((7,)), pltpu.SemaphoreType.DMA((7,)),
    ]
    anywhere = pl.BlockSpec(memory_space=pl.ANY)
    vmem = pl.BlockSpec(memory_space=pltpu.VMEM)
    output, backward, score = pl.pallas_call(
        kernel,
        out_shape=(
            jax.ShapeDtypeStruct((tokens, channels), BF16),
            jax.ShapeDtypeStruct((tokens, channels), BF16),
            jax.ShapeDtypeStruct((MODES, SPAN), F32),
        ),
        in_specs=[anywhere] * 9,
        out_specs=(vmem, vmem, vmem),
        scratch_shapes=scratch,
        compiler_params=pltpu.CompilerParams(
            collective_id=0, has_side_effects=True, vmem_limit_bytes=50 * 2**20
        ),
        cost_estimate=pl.CostEstimate(flops=2**31, bytes_accessed=2**22, transcendentals=0),
        name="chunk_convolution",
    )(query_gate, key_gate, value_input, grad_out, residues, decay, toeplitz, moments, spread)
    return (
        gated(grad_out, output),
        gated(backward, value_input),
        gated(backward, key_gate),
        score[:, :OWN].T,
    )


def solution(mesh):
    gate = P("seq", "chan")
    rows = P(("chan", "seq"), None)
    return jax.shard_map(
        body,
        mesh=mesh,
        in_specs=(gate, gate, gate, gate, rows, rows),
        out_specs=(gate, gate, gate, rows),
        check_vma=False,
    )
```

```python
import functools
import math

import jax
import jax.numpy as jnp
import ml_dtypes
import numpy as np
from jax import lax
from jax.experimental import pallas as pl
from jax.experimental.pallas import tpu as pltpu
from jax.sharding import PartitionSpec as P

MESH = pl.DeviceIdType.MESH
F32 = jnp.float32
BF16 = jnp.bfloat16
SPAN = 128
PAIR = 2 * SPAN
NODES = 16
MODES = 16
BLOCKS = 8
DEVICES = 64
CHUNKS = 32
OWN = 16
BEND = 200.0
Z_FIRST, Z_STEP = 0, 1
NEAR = 4
MOM, INN, PRM, KAP, ENT, SCO, SIB, PART, SEQ, RLY = range(10)


def scan_device(block, core):
    z = (Z_FIRST + Z_STEP * (block % 4)) % 16
    return (block // 4) * 32 + z * 2 + core


def bent(lag):
    return lag / (lag + BEND)


def bent_nodes():
    k = np.arange(NODES)
    half = bent(PAIR - 1.0) / 2.0
    return half + half * np.cos(np.pi * (2 * k + 1) / (2 * NODES))


def nodes():
    u = bent_nodes()
    return BEND * u / (1.0 - u)


def cardinal():
    u = bent_nodes()
    at = bent(np.arange(PAIR, dtype=np.float64))
    out = np.ones((NODES, PAIR))
    for k in range(NODES):
        for j in range(NODES):
            if j != k:
                out[k] *= (at - u[j]) / (u[k] - u[j])
    return out


def split(a, axis):
    high = a.astype(ml_dtypes.bfloat16)
    low = (a - high.astype(np.float64)).astype(ml_dtypes.bfloat16)
    return np.concatenate([high, low], axis=axis)


@functools.cache
def tables():
    phi = cardinal()
    t = np.arange(SPAN)
    lag = t[:, None] - t[None, :]
    inside = lag >= 0
    own = np.where(inside[None], phi[:, np.where(inside, lag, 0)], 0.0)
    cross = phi[:, lag + SPAN]
    toeplitz = np.stack([np.concatenate([a, b], axis=-1) for a, b in (
        (own, cross), (own.transpose(0, 2, 1), cross.transpose(0, 2, 1)))])
    toeplitz = toeplitz.reshape(2, NODES * SPAN, PAIR).astype(ml_dtypes.bfloat16)
    ahead, behind = phi[:, :SPAN], phi[:, SPAN:]
    moments = np.stack([np.stack([split(a, 0) for a in pair]) for pair in (
        (behind[:, ::-1], ahead), (ahead[:, ::-1], behind))])
    spread = np.stack([np.stack([split(a.T, 1) for a in pair]) for pair in (
        (ahead, behind[:, ::-1]), (behind, ahead[:, ::-1]))])
    return toeplitz, moments.reshape(4, 2 * NODES, SPAN), spread.reshape(4, SPAN, 2 * NODES)


def falling(u):
    total = jnp.full_like(u, -1.0 / 5040.0)
    for c in (720.0, -120.0, 24.0, -6.0, 2.0, -1.0):
        total = total * u - 1.0 / c
    return total * u


def kernel(
    q_hbm, k_hbm, v_hbm, go_hbm, res_hbm, dec_hbm, toe_hbm, mom_hbm, spr_hbm,
    y_out, r_out, s_out,
    q_in, k_in, v_in, go_in, res_in, dec_in, toe, mom, spr,
    x2, g2, prod, inn, y_acc, r_acc,
    part_send, part_rcv,
    mom_send, inn_send, prm_send,
    mom_rcv, inn_rcv, prm_rcv, kap_rcv, ent_rcv, sco_rcv, sib_rcv,
    psi, push, ebuf, before, ent_send, kap_send, sco_send, scalers,
    in_sem, send_sem, recv_sem,
):
    me = lax.axis_index("seq")
    core = lax.rem(me, 2)
    chip = lax.div(me, 2)
    sibling = me + 1 - 2 * core
    z = lax.rem(chip, 16)
    y_hi = lax.div(me, 32)
    ahead = lax.rem(z - Z_FIRST + 16, 16)
    scans = jnp.logical_and(lax.rem(ahead, Z_STEP) == 0, ahead < 4 * Z_STEP)
    block = y_hi * 4 + lax.rem(lax.div(ahead, Z_STEP), 4)
    own_block, own_part = lax.div(me, 8), lax.rem(me, 8)

    def scanner_of(b, c):
        return lax.div(b, 4) * 32 + lax.rem(Z_FIRST + Z_STEP * lax.rem(b, 4), 16) * 2 + c

    loads = [
        pltpu.make_async_copy(src, dst, in_sem.at[n])
        for n, (src, dst) in enumerate(
            [
                (res_hbm, res_in), (dec_hbm, dec_in),
                (k_hbm, k_in), (v_hbm, v_in), (go_hbm, go_in), (q_hbm, q_in), (mom_hbm, mom), (spr_hbm, spr), (toe_hbm, toe),
            ]
        )
    ]
    for load in loads:
        load.start()

    barrier = pltpu.get_barrier_semaphore()

    def greet(device):
        pl.semaphore_signal(barrier, inc=1, device_id={"seq": device}, device_id_type=MESH)

    @pl.when(scans)
    def _():
        def one(n, carry):
            greet(lax.rem(me + n, DEVICES))
            return carry

        lax.fori_loop(1, DEVICES, one, 0)

    @pl.when(jnp.logical_not(scans))
    def _():
        greet(sibling)
        for b in range(BLOCKS):
            for c in range(2):
                greet(scan_device(b, c))

    def push_to(src, dst, kind, device):
        return pltpu.make_async_remote_copy(
            src_ref=src, dst_ref=dst, send_sem=send_sem.at[kind], recv_sem=recv_sem.at[kind],
            device_id={"seq": device}, device_id_type=MESH,
        )

    def send(src, dst, kind, device):
        @pl.when(me != device)
        def _():
            push_to(src, dst, kind, device).start()

        @pl.when(me == device)
        def _():
            pltpu.make_async_copy(src, dst, recv_sem.at[kind]).start()

    def sent(src, dst, kind, device):
        @pl.when(me != device)
        def _():
            push_to(src, dst, kind, device).wait_send()

    def arrived(ref, kind):
        pltpu.make_async_copy(ref, ref, recv_sem.at[kind]).wait()

    loads[0].wait()
    loads[1].wait()
    lane16 = lax.broadcasted_iota(jnp.int32, (OWN, SPAN), 1)
    row16 = lax.broadcasted_iota(jnp.int32, (OWN, SPAN), 0)
    for n, ref in ((0, dec_in), (1, res_in)):
        value = ref[...]
        for r in range(2):
            wide = jnp.zeros((OWN, SPAN), F32)
            for j in range(8):
                column = jnp.broadcast_to(value[:, 8 * r + j : 8 * r + j + 1], (OWN, SPAN))
                wide = jnp.where(lane16 // 16 == j, column, wide)
            wide = jnp.where(lane16 % 16 == row16, wide, 0.0)
            prm_send[2 * n + r : 2 * n + r + 1, :] = jnp.sum(wide, axis=0, keepdims=True)

    for n in (2, 3, 4, 5, 6):
        loads[n].wait()
    x = (k_in[...].astype(F32) * v_in[...].astype(F32)).astype(BF16)
    g = (go_in[...].astype(F32) * q_in[...].astype(F32)).astype(BF16)
    x2[:SPAN, :] = x
    g2[:SPAN, :] = g

    def moment(c, value):
        both = jnp.dot(mom[2 * core + c], value, preferred_element_type=F32)
        return both[:NODES] + both[NODES:]

    of_x, of_g = moment(0, x), moment(1, g)
    first = core == 0
    part_send[...] = jnp.where(first, of_g, of_x)
    kept = jnp.where(first, of_x, of_g)

    @pl.when(scans)
    def _():
        pl.semaphore_wait(barrier, DEVICES - 1)

    @pl.when(jnp.logical_not(scans))
    def _():
        pl.semaphore_wait(barrier, 2 * BLOCKS + 1)

    param_args = [(prm_send, prm_rcv.at[own_part], PRM, scanner_of(own_block, c)) for c in range(2)]
    for args in param_args:
        send(*args)

    part = push_to(part_send, part_rcv, PART, sibling)
    part.start()

    @pl.when(first)
    def _():
        push_to(x2.at[pl.ds(0, SPAN)], x2.at[pl.ds(SPAN, SPAN)], SEQ, sibling).start()
        x2[SPAN:, :] = jnp.zeros((SPAN, x2.shape[1]), BF16)

    @pl.when(jnp.logical_not(first))
    def _():
        push_to(g2.at[pl.ds(0, SPAN)], g2.at[pl.ds(SPAN, SPAN)], SEQ, sibling).start()
        g2[SPAN:, :] = jnp.zeros((SPAN, g2.shape[1]), BF16)

    arrived(part_rcv, PART)
    total = (kept + part_rcv[...]).astype(BF16)
    for b in range(BLOCKS):
        mom_send[b] = total[:, b * SPAN : (b + 1) * SPAN]
    moment_args = [(mom_send.at[b], mom_rcv.at[chip], MOM, scan_device(b, 0) + core) for b in range(BLOCKS)]
    for args in moment_args:
        send(*args)

    loads[7].wait()
    loads[8].wait()

    @pl.when(first)
    def _():
        arrived(g2.at[pl.ds(SPAN, SPAN)], SEQ)

    @pl.when(jnp.logical_not(first))
    def _():
        arrived(x2.at[pl.ds(SPAN, SPAN)], SEQ)

    def onward(j, carry):
        cols = pl.ds(pl.multiple_of(j * 256, 256), 256)
        prod[0, :, cols] = jnp.dot(toe[0], x2[:, cols], preferred_element_type=F32)
        grad = g2[:SPAN, cols].astype(F32)
        for k in range(NODES):
            inn[k : k + 1, cols] = jnp.sum(
                prod[0, k * SPAN : (k + 1) * SPAN, cols] * grad, axis=0, keepdims=True
            )
        return carry

    lax.fori_loop(0, 4, onward, 0)
    for b in range(BLOCKS):
        inn_send[b] = inn[:, b * SPAN : (b + 1) * SPAN].astype(BF16)
    inner_args = [(inn_send.at[b], inn_rcv.at[me], INN, scan_device(b, 0)) for b in range(BLOCKS)]
    for args in inner_args:
        send(*args)

    def back(j, carry):
        cols = pl.ds(pl.multiple_of(j * 256, 256), 256)
        prod[1, :, cols] = jnp.dot(toe[1], g2[:, cols], preferred_element_type=F32)
        return carry

    lax.fori_loop(0, 4, back, 0)

    def chunk_at(i):
        return i + core * (CHUNKS - 1 - 2 * i)

    def by_z(n):
        return lax.rem(n, 2) * 16 + lax.div(n, 2)

    @pl.when(scans)
    def _():
        arrived(prm_rcv, PRM)
        lane8 = lax.broadcasted_iota(jnp.int32, (8, SPAN), 1)
        row8 = lax.broadcasted_iota(jnp.int32, (8, SPAN), 0)
        halves = []
        for r in range(4):
            packed = jnp.concatenate([prm_rcv[k, r : r + 1, :] for k in range(8)], axis=0)
            skewed = pltpu.roll(packed, 0, 1, stride=16, stride_axis=0)
            out = jnp.zeros((8, SPAN), F32)
            for j in range(8):
                turned = pltpu.roll(skewed, (SPAN - 16 * j) % SPAN, 1)
                turned = jnp.where(lane8 // 16 == row8, turned, 0.0)
                out = jnp.where(row8 == j, jnp.sum(turned, axis=0, keepdims=True), out)
            halves.append(out)
        decay = jnp.concatenate(halves[:2], axis=0)
        residue = jnp.concatenate(halves[2:], axis=0)
        scale = jnp.sqrt(falling(2.0 * decay))
        gain = residue * scale
        keep = 1.0 - falling(decay)
        points = nodes()
        for k in range(NODES):
            psi[k] = jnp.exp(decay * float(-points[k]))
        where = jnp.zeros((NODES, SPAN), F32)
        rows = lax.broadcasted_iota(jnp.int32, (NODES, SPAN), 0)
        for k in range(NODES):
            where = jnp.where(rows == k, float(-points[k]), where)
        kappa = jnp.zeros((NODES, SPAN), F32)
        for m in range(MODES):
            wave = jnp.exp(where * decay[m : m + 1, :]) * gain[m : m + 1, :]
            kappa = kappa + wave
            push[m] = wave * keep[m : m + 1, :]
        kap_send[...] = kappa.astype(BF16)
        scalers[0], scalers[1] = scale, keep

        def tell(n, carry):
            @pl.when(jnp.logical_or(lax.div(n, 2) < NEAR, lax.rem(lax.div(n, 2), 2) == core))
            def _():
                send(kap_send, kap_rcv.at[block], KAP, 2 * by_z(n) + core)

            return carry

        lax.fori_loop(0, CHUNKS, tell, 0)

        arrived(mom_rcv, MOM)

        def expand(b, carry):
            mu = mom_rcv[b].astype(F32)
            total = psi[0] * mu[0:1, :]
            for k in range(1, NODES):
                total = total + psi[k] * mu[k : k + 1, :]
            ebuf[b] = total
            return carry

        lax.fori_loop(0, CHUNKS, expand, 0)

        @pl.when(core == 1)
        def _():
            push_to(ebuf, sib_rcv, SIB, me - 1).start()

        far = jnp.exp(decay * float(-PAIR))

        def step(i, state):
            b = chunk_at(i)
            before[b] = state
            total = push[0] * state[0:1, :]
            for m in range(1, MODES):
                total = total + push[m] * state[m : m + 1, :]
            ent_send[b] = total.astype(BF16)
            return state * far + ebuf[b]

        lax.fori_loop(0, CHUNKS, step, jnp.zeros((MODES, SPAN), F32))

        def tell_entering(n, carry):
            b = by_z(n)
            send(ent_send.at[b], ent_rcv.at[core, block], ENT, 2 * b + core)

            @pl.when(lax.div(n, 2) < NEAR)
            def _():
                send(ent_send.at[b], ent_rcv.at[core, block], ENT, 2 * b + 1 - core)

            return carry

        lax.fori_loop(0, CHUNKS, tell_entering, 0)

    arrived(kap_rcv, KAP)
    passes_taps = jnp.logical_and(z >= NEAR, lax.rem(z, 2) == core)

    @pl.when(passes_taps)
    def _():
        push_to(kap_rcv, kap_rcv, KAP, sibling).start()

    def gather(b, carry):
        cols = pl.ds(pl.multiple_of(b * SPAN, SPAN), SPAN)
        kappa = kap_rcv[b].astype(F32)
        for c, acc in ((0, y_acc), (1, r_acc)):
            total = prod[c, :SPAN, cols] * kappa[0:1, :]
            for k in range(1, NODES):
                total = total + prod[c, k * SPAN : (k + 1) * SPAN, cols] * kappa[k : k + 1, :]
            acc[:, cols] = total
        return carry

    lax.fori_loop(0, BLOCKS, gather, 0)
    @pl.when(jnp.logical_and(scans, first))
    def _():
        scale, keep = scalers[0], scalers[1]
        arrived(sib_rcv, SIB)
        arrived(inn_rcv, INN)

        def cross(b, carry):
            total, inner = carry
            both = inn_rcv[2 * b].astype(F32) + inn_rcv[2 * b + 1].astype(F32)
            return total + before[b] * sib_rcv[b], inner + both

        zero = jnp.zeros((MODES, SPAN), F32)
        total, inner = lax.fori_loop(0, CHUNKS, cross, (zero, zero))
        total = total * keep
        for k in range(NODES):
            total = total + psi[k] * inner[k : k + 1, :]
        sco_send[...] = total * scale * (1.0 / math.sqrt(SPAN * DEVICES))
        for k in range(8):
            send(sco_send, sco_rcv, SCO, 8 * block + k)

    near = z < NEAR

    @pl.when(near)
    def _():
        arrived(ent_rcv, ENT)

    def relay():
        return push_to(ent_rcv.at[core], ent_rcv.at[core], RLY, sibling)

    @pl.when(jnp.logical_not(near))
    def _():
        arrived(ent_rcv.at[core], ENT)
        relay().start()
        arrived(ent_rcv.at[1 - core], RLY)

    for b in range(BLOCKS):
        cols = slice(b * SPAN, (b + 1) * SPAN)
        for c, acc, out in ((0, y_acc, y_out), (1, r_acc, r_out)):
            entering = ent_rcv[c, b]
            both = jnp.concatenate([entering, entering], axis=0)
            total = acc[:, cols] + jnp.dot(spr[2 * core + c], both, preferred_element_type=F32)
            out[:, cols] = total.astype(BF16)

    arrived(sco_rcv, SCO)
    turned = pltpu.roll(sco_rcv[...], lax.rem(SPAN - 16 * own_part, SPAN), 1)
    s_out[...] = jnp.transpose(turned)[:OWN, :]

    for args in moment_args + inner_args + param_args:
        sent(*args)
    part.wait_send()

    @pl.when(z >= NEAR)
    def _():
        relay().wait_send()

    @pl.when(passes_taps)
    def _():
        push_to(kap_rcv, kap_rcv, KAP, sibling).wait_send()

    @pl.when(first)
    def _():
        push_to(x2.at[pl.ds(0, SPAN)], x2.at[pl.ds(SPAN, SPAN)], SEQ, sibling).wait_send()

    @pl.when(jnp.logical_not(first))
    def _():
        push_to(g2.at[pl.ds(0, SPAN)], g2.at[pl.ds(SPAN, SPAN)], SEQ, sibling).wait_send()

    @pl.when(scans)
    def _():
        def told(n, carry):
            @pl.when(jnp.logical_or(lax.div(n, 2) < NEAR, lax.rem(lax.div(n, 2), 2) == core))
            def _():
                sent(kap_send, kap_rcv.at[block], KAP, 2 * by_z(n) + core)

            return carry

        lax.fori_loop(0, CHUNKS, told, 0)

        def stepped(n, carry):
            b = by_z(n)
            sent(ent_send.at[b], ent_rcv.at[core, block], ENT, 2 * b + core)

            @pl.when(lax.div(n, 2) < NEAR)
            def _():
                sent(ent_send.at[b], ent_rcv.at[core, block], ENT, 2 * b + 1 - core)

            return carry

        lax.fori_loop(0, CHUNKS, stepped, 0)

        @pl.when(core == 1)
        def _():
            push_to(ebuf, sib_rcv, SIB, me - 1).wait_send()

        @pl.when(core == 0)
        def _():
            for k in range(8):
                sent(sco_send, sco_rcv, SCO, 8 * block + k)


def gated(left, right):
    return (left.astype(F32) * right.astype(F32)).astype(BF16)


def body(query_gate, key_gate, value_input, grad_out, residues, decay):
    toeplitz, moments, spread = (jnp.asarray(t) for t in tables())
    tokens, channels = query_gate.shape
    vm = pltpu.VMEM
    gate = vm((tokens, channels), BF16)
    scratch = [
        gate, gate, gate, gate, vm((OWN, MODES), F32), vm((OWN, MODES), F32),
        vm(toeplitz.shape, BF16), vm(moments.shape, BF16), vm(spread.shape, BF16),
        vm((PAIR, channels), BF16), vm((PAIR, channels), BF16),
        vm((2, NODES * SPAN, channels), F32), vm((NODES, channels), F32),
        vm((tokens, channels), F32), vm((tokens, channels), F32),
        vm((NODES, channels), F32), vm((NODES, channels), F32),
        vm((BLOCKS, NODES, SPAN), BF16), vm((BLOCKS, NODES, SPAN), BF16), vm((4, SPAN), F32),
        vm((CHUNKS, NODES, SPAN), BF16), vm((DEVICES, NODES, SPAN), BF16), vm((8, 4, SPAN), F32),
        vm((BLOCKS, NODES, SPAN), BF16), vm((2, BLOCKS, NODES, SPAN), BF16), vm((MODES, SPAN), F32),
        vm((CHUNKS, MODES, SPAN), F32),
        vm((NODES, MODES, SPAN), F32), vm((MODES, NODES, SPAN), F32), vm((CHUNKS, MODES, SPAN), F32),
        vm((CHUNKS, MODES, SPAN), F32), vm((CHUNKS, NODES, SPAN), BF16), vm((NODES, SPAN), BF16),
        vm((MODES, SPAN), F32), vm((2, MODES, SPAN), F32),
        pltpu.SemaphoreType.DMA((9,)), pltpu.SemaphoreType.DMA((10,)), pltpu.SemaphoreType.DMA((10,)),
    ]
    hbm = pl.BlockSpec(memory_space=pltpu.HBM)
    vmem = pl.BlockSpec(memory_space=pltpu.VMEM)
    output, backward, score = pl.pallas_call(
        kernel,
        out_shape=(
            jax.ShapeDtypeStruct((tokens, channels), BF16),
            jax.ShapeDtypeStruct((tokens, channels), BF16),
            jax.ShapeDtypeStruct((OWN, MODES), F32),
        ),
        in_specs=[hbm] * 9,
        out_specs=(vmem, vmem, vmem),
        scratch_shapes=scratch,
        compiler_params=pltpu.CompilerParams(
            collective_id=0, has_side_effects=True, vmem_limit_bytes=48 * 2**20
        ),
        cost_estimate=pl.CostEstimate(flops=2**31, bytes_accessed=2**22, transcendentals=0),
        name="chunk_convolution",
    )(*(pltpu.with_memory_space_constraint(a, pltpu.HBM) for a in (
        query_gate, key_gate, value_input, grad_out, residues, decay, toeplitz, moments, spread)))
    return (
        gated(grad_out, output),
        gated(backward, value_input),
        gated(backward, key_gate),
        score,
    )


def solution(mesh):
    gate = P("seq", "chan")
    rows = P(("chan", "seq"), None)
    return jax.shard_map(
        body,
        mesh=mesh,
        in_specs=(gate, gate, gate, gate, rows, rows),
        out_specs=(gate, gate, gate, rows),
        check_vma=False,
    )
```

```python
import functools
import math

import jax
import jax.numpy as jnp
import ml_dtypes
import numpy as np
from jax import lax
from jax.experimental import pallas as pl
from jax.experimental.pallas import tpu as pltpu
from jax.sharding import PartitionSpec as P

MESH = pl.DeviceIdType.MESH
F32 = jnp.float32
BF16 = jnp.bfloat16
SPAN = 128
PAIR = 2 * SPAN
NODES = 16
MODES = 16
BLOCKS = 8
DEVICES = 64
CHUNKS = 32
OWN = 16
BEND = 200.0
Z_FIRST, Z_STEP = 0, 1
NEAR = 4
MOM, INN, PRM, KAP, ENT, SCO, SIB, PART, SEQ, RLY, HALF = range(11)


def scan_device(block, core):
    z = (Z_FIRST + Z_STEP * (block % 4)) % 16
    return (block // 4) * 32 + z * 2 + core


def bent(lag):
    return lag / (lag + BEND)


def bent_nodes():
    k = np.arange(NODES)
    half = bent(PAIR - 1.0) / 2.0
    return half + half * np.cos(np.pi * (2 * k + 1) / (2 * NODES))


def nodes():
    u = bent_nodes()
    return BEND * u / (1.0 - u)


def cardinal():
    u = bent_nodes()
    at = bent(np.arange(PAIR, dtype=np.float64))
    out = np.ones((NODES, PAIR))
    for k in range(NODES):
        for j in range(NODES):
            if j != k:
                out[k] *= (at - u[j]) / (u[k] - u[j])
    return out


def split(a, axis):
    high = a.astype(ml_dtypes.bfloat16)
    low = (a - high.astype(np.float64)).astype(ml_dtypes.bfloat16)
    return np.concatenate([high, low], axis=axis)


@functools.cache
def tables():
    phi = cardinal()
    t = np.arange(SPAN)
    lag = t[:, None] - t[None, :]
    inside = lag >= 0
    own = np.where(inside[None], phi[:, np.where(inside, lag, 0)], 0.0)
    cross = phi[:, lag + SPAN]
    toeplitz = np.stack([np.concatenate([a, b], axis=-1) for a, b in (
        (own, cross), (own.transpose(0, 2, 1), cross.transpose(0, 2, 1)))])
    toeplitz = toeplitz.reshape(2, NODES * SPAN, PAIR).astype(ml_dtypes.bfloat16)
    ahead, behind = phi[:, :SPAN], phi[:, SPAN:]
    moments = np.stack([np.stack([split(a, 0) for a in pair]) for pair in (
        (behind[:, ::-1], ahead), (ahead[:, ::-1], behind))])
    spread = np.stack([np.stack([split(a.T, 1) for a in pair]) for pair in (
        (ahead, behind[:, ::-1]), (behind, ahead[:, ::-1]))])
    return toeplitz, moments.reshape(4, 2 * NODES, SPAN), spread.reshape(4, SPAN, 2 * NODES)


def falling(u):
    total = jnp.full_like(u, -1.0 / 5040.0)
    for c in (720.0, -120.0, 24.0, -6.0, 2.0, -1.0):
        total = total * u - 1.0 / c
    return total * u


def kernel(
    q_hbm, k_hbm, v_hbm, go_hbm, res_hbm, dec_hbm, toe_hbm, mom_hbm, spr_hbm,
    y_out, r_out, s_out,
    q_in, k_in, v_in, go_in, res_in, dec_in, toe, mom, spr,
    x2, g2, prod, inn, y_acc, r_acc,
    part_send, part_rcv, half_rcv,
    mom_send, inn_send, prm_send,
    mom_rcv, inn_rcv, prm_rcv, kap_rcv, ent_rcv, sco_rcv, sib_rcv,
    psi, push, ebuf, before, ent_send, kap_send, sco_send, scalers,
    in_sem, send_sem, recv_sem,
):
    me = lax.axis_index("seq")
    core = lax.rem(me, 2)
    chip = lax.div(me, 2)
    sibling = me + 1 - 2 * core
    z = lax.rem(chip, 16)
    y_hi = lax.div(me, 32)
    ahead = lax.rem(z - Z_FIRST + 16, 16)
    scans = jnp.logical_and(lax.rem(ahead, Z_STEP) == 0, ahead < 4 * Z_STEP)
    block = y_hi * 4 + lax.rem(lax.div(ahead, Z_STEP), 4)
    own_block, own_part = lax.div(me, 8), lax.rem(me, 8)

    def scanner_of(b, c):
        return lax.div(b, 4) * 32 + lax.rem(Z_FIRST + Z_STEP * lax.rem(b, 4), 16) * 2 + c

    loads = [
        pltpu.make_async_copy(src, dst, in_sem.at[n])
        for n, (src, dst) in enumerate(
            [
                (res_hbm, res_in), (dec_hbm, dec_in),
                (k_hbm, k_in), (v_hbm, v_in), (go_hbm, go_in), (q_hbm, q_in), (mom_hbm, mom), (spr_hbm, spr), (toe_hbm, toe),
            ]
        )
    ]
    for load in loads:
        load.start()

    barrier = pltpu.get_barrier_semaphore()

    def greet(device):
        pl.semaphore_signal(barrier, inc=1, device_id={"seq": device}, device_id_type=MESH)

    @pl.when(scans)
    def _():
        for b in range(BLOCKS):
            for c in range(2):
                device = scan_device(b, c)

                @pl.when(me != device)
                def _():
                    greet(device)

        def one(n, carry):
            z_there = lax.rem(Z_FIRST + 4 + lax.rem(lax.div(n, 4) + 4, 12), 16)
            greet(lax.rem(n, 4) // 2 * 32 + z_there * 2 + lax.rem(n, 2))
            return carry

        lax.fori_loop(0, DEVICES - 2 * BLOCKS, one, 0)
        pl.semaphore_wait(barrier, 2 * BLOCKS - 1)

    @pl.when(jnp.logical_not(scans))
    def _():
        greet(sibling)

    def push_to(src, dst, kind, device):
        return pltpu.make_async_remote_copy(
            src_ref=src, dst_ref=dst, send_sem=send_sem.at[kind], recv_sem=recv_sem.at[kind],
            device_id={"seq": device}, device_id_type=MESH,
        )

    def send(src, dst, kind, device):
        @pl.when(me != device)
        def _():
            push_to(src, dst, kind, device).start()

        @pl.when(me == device)
        def _():
            pltpu.make_async_copy(src, dst, recv_sem.at[kind]).start()

    def sent(src, dst, kind, device):
        @pl.when(me != device)
        def _():
            push_to(src, dst, kind, device).wait_send()

    def arrived(ref, kind):
        pltpu.make_async_copy(ref, ref, recv_sem.at[kind]).wait()

    loads[0].wait()
    loads[1].wait()
    lane16 = lax.broadcasted_iota(jnp.int32, (OWN, SPAN), 1)
    row16 = lax.broadcasted_iota(jnp.int32, (OWN, SPAN), 0)
    for n, ref in ((0, dec_in), (1, res_in)):
        value = ref[...]
        for r in range(2):
            wide = jnp.zeros((OWN, SPAN), F32)
            for j in range(8):
                column = jnp.broadcast_to(value[:, 8 * r + j : 8 * r + j + 1], (OWN, SPAN))
                wide = jnp.where(lane16 // 16 == j, column, wide)
            wide = jnp.where(lane16 % 16 == row16, wide, 0.0)
            prm_send[2 * n + r : 2 * n + r + 1, :] = jnp.sum(wide, axis=0, keepdims=True)

    for n in (2, 3, 4, 5, 6):
        loads[n].wait()
    x = (k_in[...].astype(F32) * v_in[...].astype(F32)).astype(BF16)
    g = (go_in[...].astype(F32) * q_in[...].astype(F32)).astype(BF16)
    x2[:SPAN, :] = x
    g2[:SPAN, :] = g

    def moment(c, value):
        both = jnp.dot(mom[2 * core + c], value, preferred_element_type=F32)
        return both[:NODES] + both[NODES:]

    of_x, of_g = moment(0, x), moment(1, g)
    first = core == 0
    part_send[...] = jnp.where(first, of_g, of_x)
    kept = jnp.where(first, of_x, of_g)

    @pl.when(jnp.logical_not(scans))
    def _():
        pl.semaphore_wait(barrier, 2 * BLOCKS + 1)

    param_args = [(prm_send, prm_rcv.at[own_part], PRM, scanner_of(own_block, c)) for c in range(2)]
    for args in param_args:
        send(*args)

    part = push_to(part_send, part_rcv, PART, sibling)
    part.start()

    @pl.when(first)
    def _():
        push_to(x2.at[pl.ds(0, SPAN)], x2.at[pl.ds(SPAN, SPAN)], SEQ, sibling).start()
        x2[SPAN:, :] = jnp.zeros((SPAN, x2.shape[1]), BF16)

    @pl.when(jnp.logical_not(first))
    def _():
        push_to(g2.at[pl.ds(0, SPAN)], g2.at[pl.ds(SPAN, SPAN)], SEQ, sibling).start()
        g2[SPAN:, :] = jnp.zeros((SPAN, g2.shape[1]), BF16)

    arrived(part_rcv, PART)
    total = (kept + part_rcv[...]).astype(BF16)
    for b in range(BLOCKS):
        mom_send[b] = total[:, b * SPAN : (b + 1) * SPAN]
    moment_args = [(mom_send.at[b], mom_rcv.at[chip], MOM, scan_device(b, 0) + core) for b in range(BLOCKS)]
    for args in moment_args:
        send(*args)

    @pl.when(jnp.logical_not(scans))
    def _():
        for b in range(BLOCKS):
            for c in range(2):
                greet(scan_device(b, c))


    loads[7].wait()
    loads[8].wait()

    @pl.when(first)
    def _():
        arrived(g2.at[pl.ds(SPAN, SPAN)], SEQ)

    @pl.when(jnp.logical_not(first))
    def _():
        arrived(x2.at[pl.ds(SPAN, SPAN)], SEQ)

    def onward(j, carry):
        cols = pl.ds(pl.multiple_of(j * 256, 256), 256)
        prod[0, :, cols] = jnp.dot(toe[0], x2[:, cols], preferred_element_type=F32)
        grad = g2[:SPAN, cols].astype(F32)
        for k in range(NODES):
            inn[k : k + 1, cols] = jnp.sum(
                prod[0, k * SPAN : (k + 1) * SPAN, cols] * grad, axis=0, keepdims=True
            )
        return carry

    lax.fori_loop(0, 4, onward, 0)
    wide = BLOCKS // 2 * SPAN
    mine = pl.ds(pl.multiple_of(core * wide, wide), wide)
    other = pl.ds(pl.multiple_of((1 - core) * wide, wide), wide)
    half = push_to(inn.at[:, other], half_rcv, HALF, sibling)
    half.start()
    arrived(half_rcv, HALF)
    inner = inn[:, mine] + half_rcv[...]
    for b in range(BLOCKS // 2):
        inn_send[b] = inner[:, b * SPAN : (b + 1) * SPAN].astype(BF16)
    inner_args = [
        (inn_send.at[b], inn_rcv.at[chip], INN, scanner_of(core * (BLOCKS // 2) + b, 0))
        for b in range(BLOCKS // 2)
    ]
    for args in inner_args:
        send(*args)

    def back(j, carry):
        cols = pl.ds(pl.multiple_of(j * 256, 256), 256)
        prod[1, :, cols] = jnp.dot(toe[1], g2[:, cols], preferred_element_type=F32)
        return carry

    lax.fori_loop(0, 4, back, 0)

    def chunk_at(i):
        return i + core * (CHUNKS - 1 - 2 * i)

    def by_z(n):
        return lax.rem(n, 2) * 16 + lax.div(n, 2)

    @pl.when(scans)
    def _():
        arrived(prm_rcv, PRM)
        lane8 = lax.broadcasted_iota(jnp.int32, (8, SPAN), 1)
        row8 = lax.broadcasted_iota(jnp.int32, (8, SPAN), 0)
        halves = []
        for r in range(4):
            packed = jnp.concatenate([prm_rcv[k, r : r + 1, :] for k in range(8)], axis=0)
            skewed = pltpu.roll(packed, 0, 1, stride=16, stride_axis=0)
            out = jnp.zeros((8, SPAN), F32)
            for j in range(8):
                turned = pltpu.roll(skewed, (SPAN - 16 * j) % SPAN, 1)
                turned = jnp.where(lane8 // 16 == row8, turned, 0.0)
                out = jnp.where(row8 == j, jnp.sum(turned, axis=0, keepdims=True), out)
            halves.append(out)
        decay = jnp.concatenate(halves[:2], axis=0)
        residue = jnp.concatenate(halves[2:], axis=0)
        scale = jnp.sqrt(falling(2.0 * decay))
        gain = residue * scale
        keep = 1.0 - falling(decay)
        points = nodes()
        for k in range(NODES):
            psi[k] = jnp.exp(decay * float(-points[k]))
        where = jnp.zeros((NODES, SPAN), F32)
        rows = lax.broadcasted_iota(jnp.int32, (NODES, SPAN), 0)
        for k in range(NODES):
            where = jnp.where(rows == k, float(-points[k]), where)
        kappa = jnp.zeros((NODES, SPAN), F32)
        for m in range(MODES):
            wave = jnp.exp(where * decay[m : m + 1, :]) * gain[m : m + 1, :]
            kappa = kappa + wave
            push[m] = wave * keep[m : m + 1, :]
        kap_send[...] = kappa.astype(BF16)
        scalers[0], scalers[1] = scale, keep

        pl.semaphore_wait(barrier, DEVICES - 2 * BLOCKS)

        def tell(n, carry):
            @pl.when(jnp.logical_or(lax.div(n, 2) < NEAR, lax.rem(lax.div(n, 2), 2) == core))
            def _():
                send(kap_send, kap_rcv.at[block], KAP, 2 * by_z(n) + core)

            return carry

        lax.fori_loop(0, CHUNKS, tell, 0)

        arrived(mom_rcv, MOM)

        def expand(b, carry):
            mu = mom_rcv[b].astype(F32)
            total = psi[0] * mu[0:1, :]
            for k in range(1, NODES):
                total = total + psi[k] * mu[k : k + 1, :]
            ebuf[b] = total
            return carry

        lax.fori_loop(0, CHUNKS, expand, 0, unroll=4)

        @pl.when(core == 1)
        def _():
            push_to(ebuf, sib_rcv, SIB, me - 1).start()

        far = jnp.exp(decay * float(-PAIR))

        def step(i, state):
            b = chunk_at(i)
            before[b] = state
            total = push[0] * state[0:1, :]
            for m in range(1, MODES):
                total = total + push[m] * state[m : m + 1, :]
            ent_send[b] = total.astype(BF16)
            return state * far + ebuf[b]

        lax.fori_loop(0, CHUNKS, step, jnp.zeros((MODES, SPAN), F32), unroll=4)

        def tell_entering(n, carry):
            b = by_z(n)
            send(ent_send.at[b], ent_rcv.at[core, block], ENT, 2 * b + core)

            @pl.when(lax.div(n, 2) < NEAR)
            def _():
                send(ent_send.at[b], ent_rcv.at[core, block], ENT, 2 * b + 1 - core)

            return carry

        lax.fori_loop(0, CHUNKS, tell_entering, 0)

    arrived(kap_rcv, KAP)
    passes_taps = jnp.logical_and(z >= NEAR, lax.rem(z, 2) == core)

    @pl.when(passes_taps)
    def _():
        push_to(kap_rcv, kap_rcv, KAP, sibling).start()

    def gather(b, carry):
        cols = pl.ds(pl.multiple_of(b * SPAN, SPAN), SPAN)
        kappa = kap_rcv[b].astype(F32)
        for c, acc in ((0, y_acc), (1, r_acc)):
            total = prod[c, :SPAN, cols] * kappa[0:1, :]
            for k in range(1, NODES):
                total = total + prod[c, k * SPAN : (k + 1) * SPAN, cols] * kappa[k : k + 1, :]
            acc[:, cols] = total
        return carry

    lax.fori_loop(0, BLOCKS, gather, 0)
    @pl.when(jnp.logical_and(scans, first))
    def _():
        scale, keep = scalers[0], scalers[1]
        arrived(sib_rcv, SIB)
        arrived(inn_rcv, INN)

        def cross(b, carry):
            total, inner = carry
            return total + before[b] * sib_rcv[b], inner + inn_rcv[b].astype(F32)

        zero = jnp.zeros((MODES, SPAN), F32)
        total, inner = lax.fori_loop(0, CHUNKS, cross, (zero, zero), unroll=4)
        total = total * keep
        for k in range(NODES):
            total = total + psi[k] * inner[k : k + 1, :]
        sco_send[...] = total * scale * (1.0 / math.sqrt(SPAN * DEVICES))
        for k in range(8):
            send(sco_send, sco_rcv, SCO, 8 * block + k)

    near = z < NEAR

    @pl.when(near)
    def _():
        arrived(ent_rcv, ENT)

    def relay():
        return push_to(ent_rcv.at[core], ent_rcv.at[core], RLY, sibling)

    @pl.when(jnp.logical_not(near))
    def _():
        arrived(ent_rcv.at[core], ENT)
        relay().start()
        arrived(ent_rcv.at[1 - core], RLY)

    for b in range(BLOCKS):
        cols = slice(b * SPAN, (b + 1) * SPAN)
        for c, acc, out in ((0, y_acc, y_out), (1, r_acc, r_out)):
            entering = ent_rcv[c, b]
            both = jnp.concatenate([entering, entering], axis=0)
            total = acc[:, cols] + jnp.dot(spr[2 * core + c], both, preferred_element_type=F32)
            out[:, cols] = total.astype(BF16)

    arrived(sco_rcv, SCO)
    turned = pltpu.roll(sco_rcv[...], lax.rem(SPAN - 16 * own_part, SPAN), 1)
    s_out[...] = jnp.transpose(turned)[:OWN, :]

    for args in moment_args + inner_args + param_args:
        sent(*args)
    part.wait_send()
    half.wait_send()

    @pl.when(z >= NEAR)
    def _():
        relay().wait_send()

    @pl.when(passes_taps)
    def _():
        push_to(kap_rcv, kap_rcv, KAP, sibling).wait_send()

    @pl.when(first)
    def _():
        push_to(x2.at[pl.ds(0, SPAN)], x2.at[pl.ds(SPAN, SPAN)], SEQ, sibling).wait_send()

    @pl.when(jnp.logical_not(first))
    def _():
        push_to(g2.at[pl.ds(0, SPAN)], g2.at[pl.ds(SPAN, SPAN)], SEQ, sibling).wait_send()

    @pl.when(scans)
    def _():
        def told(n, carry):
            @pl.when(jnp.logical_or(lax.div(n, 2) < NEAR, lax.rem(lax.div(n, 2), 2) == core))
            def _():
                sent(kap_send, kap_rcv.at[block], KAP, 2 * by_z(n) + core)

            return carry

        lax.fori_loop(0, CHUNKS, told, 0)

        def stepped(n, carry):
            b = by_z(n)
            sent(ent_send.at[b], ent_rcv.at[core, block], ENT, 2 * b + core)

            @pl.when(lax.div(n, 2) < NEAR)
            def _():
                sent(ent_send.at[b], ent_rcv.at[core, block], ENT, 2 * b + 1 - core)

            return carry

        lax.fori_loop(0, CHUNKS, stepped, 0)

        @pl.when(core == 1)
        def _():
            push_to(ebuf, sib_rcv, SIB, me - 1).wait_send()

        @pl.when(core == 0)
        def _():
            for k in range(8):
                sent(sco_send, sco_rcv, SCO, 8 * block + k)


def gated(left, right):
    return (left.astype(F32) * right.astype(F32)).astype(BF16)


def body(query_gate, key_gate, value_input, grad_out, residues, decay):
    toeplitz, moments, spread = (jnp.asarray(t) for t in tables())
    tokens, channels = query_gate.shape
    vm = pltpu.VMEM
    gate = vm((tokens, channels), BF16)
    scratch = [
        gate, gate, gate, gate, vm((OWN, MODES), F32), vm((OWN, MODES), F32),
        vm(toeplitz.shape, BF16), vm(moments.shape, BF16), vm(spread.shape, BF16),
        vm((PAIR, channels), BF16), vm((PAIR, channels), BF16),
        vm((2, NODES * SPAN, channels), F32), vm((NODES, channels), F32),
        vm((tokens, channels), F32), vm((tokens, channels), F32),
        vm((NODES, channels), F32), vm((NODES, channels), F32), vm((NODES, channels // 2), F32),
        vm((BLOCKS, NODES, SPAN), BF16), vm((BLOCKS // 2, NODES, SPAN), BF16), vm((4, SPAN), F32),
        vm((CHUNKS, NODES, SPAN), BF16), vm((CHUNKS, NODES, SPAN), BF16), vm((8, 4, SPAN), F32),
        vm((BLOCKS, NODES, SPAN), BF16), vm((2, BLOCKS, NODES, SPAN), BF16), vm((MODES, SPAN), F32),
        vm((CHUNKS, MODES, SPAN), F32),
        vm((NODES, MODES, SPAN), F32), vm((MODES, NODES, SPAN), F32), vm((CHUNKS, MODES, SPAN), F32),
        vm((CHUNKS, MODES, SPAN), F32), vm((CHUNKS, NODES, SPAN), BF16), vm((NODES, SPAN), BF16),
        vm((MODES, SPAN), F32), vm((2, MODES, SPAN), F32),
        pltpu.SemaphoreType.DMA((9,)), pltpu.SemaphoreType.DMA((11,)), pltpu.SemaphoreType.DMA((11,)),
    ]
    hbm = pl.BlockSpec(memory_space=pltpu.HBM)
    vmem = pl.BlockSpec(memory_space=pltpu.VMEM)
    output, backward, score = pl.pallas_call(
        kernel,
        out_shape=(
            jax.ShapeDtypeStruct((tokens, channels), BF16),
            jax.ShapeDtypeStruct((tokens, channels), BF16),
            jax.ShapeDtypeStruct((OWN, MODES), F32),
        ),
        in_specs=[hbm] * 9,
        out_specs=(vmem, vmem, vmem),
        scratch_shapes=scratch,
        compiler_params=pltpu.CompilerParams(
            collective_id=0, has_side_effects=True, vmem_limit_bytes=48 * 2**20
        ),
        cost_estimate=pl.CostEstimate(flops=2**31, bytes_accessed=2**22, transcendentals=0),
        name="chunk_convolution",
    )(*(pltpu.with_memory_space_constraint(a, pltpu.HBM) for a in (
        query_gate, key_gate, value_input, grad_out, residues, decay, toeplitz, moments, spread)))
    return (
        gated(grad_out, output),
        gated(backward, value_input),
        gated(backward, key_gate),
        score,
    )


def solution(mesh):
    gate = P("seq", "chan")
    rows = P(("chan", "seq"), None)
    return jax.shard_map(
        body,
        mesh=mesh,
        in_specs=(gate, gate, gate, gate, rows, rows),
        out_specs=(gate, gate, gate, rows),
        check_vma=False,
    )
```

```python
import functools
import math

import jax
import jax.numpy as jnp
import ml_dtypes
import numpy as np
from jax import lax
from jax.experimental import pallas as pl
from jax.experimental.pallas import tpu as pltpu
from jax.sharding import PartitionSpec as P

MESH = pl.DeviceIdType.MESH
F32 = jnp.float32
BF16 = jnp.bfloat16
SPAN = 128
PAIR = 2 * SPAN
NODES = 16
MODES = 16
BLOCKS = 8
DEVICES = 64
CHUNKS = 32
OWN = 16
BEND = 200.0
Z_FIRST, Z_STEP = 0, 1
NEAR = 4
MOM, INN, PRM, KAP, ENT, SCO, SIB, PART, SEQ, RLY, HALF = range(11)


def scan_device(block, core):
    z = (Z_FIRST + Z_STEP * (block % 4)) % 16
    return (block // 4) * 32 + z * 2 + core


def bent(lag):
    return lag / (lag + BEND)


def bent_nodes():
    k = np.arange(NODES)
    half = bent(PAIR - 1.0) / 2.0
    return half + half * np.cos(np.pi * (2 * k + 1) / (2 * NODES))


def nodes():
    u = bent_nodes()
    return BEND * u / (1.0 - u)


def cardinal():
    u = bent_nodes()
    at = bent(np.arange(PAIR, dtype=np.float64))
    out = np.ones((NODES, PAIR))
    for k in range(NODES):
        for j in range(NODES):
            if j != k:
                out[k] *= (at - u[j]) / (u[k] - u[j])
    return out


def split(a, axis):
    high = a.astype(ml_dtypes.bfloat16)
    low = (a - high.astype(np.float64)).astype(ml_dtypes.bfloat16)
    return np.concatenate([high, low], axis=axis)


@functools.cache
def tables():
    phi = cardinal()
    t = np.arange(SPAN)
    lag = t[:, None] - t[None, :]
    inside = lag >= 0
    own = np.where(inside[None], phi[:, np.where(inside, lag, 0)], 0.0)
    cross = phi[:, lag + SPAN]
    toeplitz = np.stack([np.concatenate([a, b], axis=-1) for a, b in (
        (own, cross), (own.transpose(0, 2, 1), cross.transpose(0, 2, 1)))])
    toeplitz = toeplitz.reshape(2, NODES * SPAN, PAIR).astype(ml_dtypes.bfloat16)
    ahead, behind = phi[:, :SPAN], phi[:, SPAN:]
    moments = np.stack([np.stack([split(a, 0) for a in pair]) for pair in (
        (behind[:, ::-1], ahead), (ahead[:, ::-1], behind))])
    spread = np.stack([np.stack([split(a.T, 1) for a in pair]) for pair in (
        (ahead, behind[:, ::-1]), (behind, ahead[:, ::-1]))])
    return toeplitz, moments.reshape(4, 2 * NODES, SPAN), spread.reshape(4, SPAN, 2 * NODES)


def falling(u):
    total = jnp.full_like(u, -1.0 / 5040.0)
    for c in (720.0, -120.0, 24.0, -6.0, 2.0, -1.0):
        total = total * u - 1.0 / c
    return total * u


def kernel(
    q_hbm, k_hbm, v_hbm, go_hbm, res_hbm, dec_hbm, toe_hbm, mom_hbm, spr_hbm,
    y_out, r_out, s_out,
    q_in, k_in, v_in, go_in, res_in, dec_in, toe, mom, spr,
    x2, g2, prod, inn, y_acc, r_acc,
    part_send, part_rcv, half_rcv,
    mom_send, inn_send, prm_send,
    mom_rcv, inn_rcv, prm_rcv, kap_rcv, ent_rcv, sco_rcv, sib_rcv,
    psi, push, ebuf, before, ent_send, kap_send, sco_send, scalers,
    in_sem, send_sem, recv_sem,
):
    me = lax.axis_index("seq")
    core = lax.rem(me, 2)
    chip = lax.div(me, 2)
    sibling = me + 1 - 2 * core
    z = lax.rem(chip, 16)
    y_hi = lax.div(me, 32)
    ahead = lax.rem(z - Z_FIRST + 16, 16)
    scans = jnp.logical_and(lax.rem(ahead, Z_STEP) == 0, ahead < 4 * Z_STEP)
    block = y_hi * 4 + lax.rem(lax.div(ahead, Z_STEP), 4)
    own_block, own_part = lax.div(me, 8), lax.rem(me, 8)

    def scanner_of(b, c):
        return lax.div(b, 4) * 32 + lax.rem(Z_FIRST + Z_STEP * lax.rem(b, 4), 16) * 2 + c

    loads = [
        pltpu.make_async_copy(src, dst, in_sem.at[n])
        for n, (src, dst) in enumerate(
            [
                (res_hbm, res_in), (dec_hbm, dec_in),
                (k_hbm, k_in), (v_hbm, v_in), (go_hbm, go_in), (q_hbm, q_in), (mom_hbm, mom), (spr_hbm, spr), (toe_hbm, toe),
            ]
        )
    ]
    for load in loads:
        load.start()

    barrier = pltpu.get_barrier_semaphore()

    def greet(device):
        pl.semaphore_signal(barrier, inc=1, device_id={"seq": device}, device_id_type=MESH)

    @pl.when(scans)
    def _():
        for b in range(BLOCKS):
            for c in range(2):
                device = scan_device(b, c)

                @pl.when(me != device)
                def _():
                    greet(device)

        def one(n, carry):
            z_there = lax.rem(Z_FIRST + 4 + lax.rem(lax.div(n, 4) + 4, 12), 16)
            greet(lax.rem(n, 4) // 2 * 32 + z_there * 2 + lax.rem(n, 2))
            return carry

        lax.fori_loop(0, DEVICES - 2 * BLOCKS, one, 0)
        pl.semaphore_wait(barrier, 2 * BLOCKS - 1)

    @pl.when(jnp.logical_not(scans))
    def _():
        greet(sibling)

    def push_to(src, dst, kind, device):
        return pltpu.make_async_remote_copy(
            src_ref=src, dst_ref=dst, send_sem=send_sem.at[kind], recv_sem=recv_sem.at[kind],
            device_id={"seq": device}, device_id_type=MESH,
        )

    def send(src, dst, kind, device):
        @pl.when(me != device)
        def _():
            push_to(src, dst, kind, device).start()

        @pl.when(me == device)
        def _():
            pltpu.make_async_copy(src, dst, recv_sem.at[kind]).start()

    def sent(src, dst, kind, device):
        @pl.when(me != device)
        def _():
            push_to(src, dst, kind, device).wait_send()

    def arrived(ref, kind):
        pltpu.make_async_copy(ref, ref, recv_sem.at[kind]).wait()

    loads[0].wait()
    loads[1].wait()
    lane16 = lax.broadcasted_iota(jnp.int32, (OWN, SPAN), 1)
    row16 = lax.broadcasted_iota(jnp.int32, (OWN, SPAN), 0)
    for n, ref in ((0, dec_in), (1, res_in)):
        value = ref[...]
        for r in range(2):
            wide = jnp.zeros((OWN, SPAN), F32)
            for j in range(8):
                column = jnp.broadcast_to(value[:, 8 * r + j : 8 * r + j + 1], (OWN, SPAN))
                wide = jnp.where(lane16 // 16 == j, column, wide)
            wide = jnp.where(lane16 % 16 == row16, wide, 0.0)
            prm_send[2 * n + r : 2 * n + r + 1, :] = jnp.sum(wide, axis=0, keepdims=True)

    for n in (2, 3, 4, 5, 6):
        loads[n].wait()
    x = (k_in[...].astype(F32) * v_in[...].astype(F32)).astype(BF16)
    g = (go_in[...].astype(F32) * q_in[...].astype(F32)).astype(BF16)
    x2[:SPAN, :] = x
    g2[:SPAN, :] = g

    def moment(c, value):
        both = jnp.dot(mom[2 * core + c], value, preferred_element_type=F32)
        return both[:NODES] + both[NODES:]

    of_x, of_g = moment(0, x), moment(1, g)
    first = core == 0
    part_send[...] = jnp.where(first, of_g, of_x)
    kept = jnp.where(first, of_x, of_g)

    @pl.when(jnp.logical_not(scans))
    def _():
        pl.semaphore_wait(barrier, 2 * BLOCKS + 1)

    param_args = [(prm_send, prm_rcv.at[own_part], PRM, scanner_of(own_block, c)) for c in range(2)]
    for args in param_args:
        send(*args)

    part = push_to(part_send, part_rcv, PART, sibling)
    part.start()

    @pl.when(first)
    def _():
        push_to(x2.at[pl.ds(0, SPAN)], x2.at[pl.ds(SPAN, SPAN)], SEQ, sibling).start()
        x2[SPAN:, :] = jnp.zeros((SPAN, x2.shape[1]), BF16)

    @pl.when(jnp.logical_not(first))
    def _():
        push_to(g2.at[pl.ds(0, SPAN)], g2.at[pl.ds(SPAN, SPAN)], SEQ, sibling).start()
        g2[SPAN:, :] = jnp.zeros((SPAN, g2.shape[1]), BF16)

    arrived(part_rcv, PART)
    total = (kept + part_rcv[...]).astype(BF16)
    for b in range(BLOCKS):
        mom_send[b] = total[:, b * SPAN : (b + 1) * SPAN]
    moment_args = [(mom_send.at[b], mom_rcv.at[chip], MOM, scan_device(b, 0) + core) for b in range(BLOCKS)]
    for args in moment_args:
        send(*args)

    @pl.when(jnp.logical_not(scans))
    def _():
        for b in range(BLOCKS):
            for c in range(2):
                greet(scan_device(b, c))


    loads[7].wait()
    loads[8].wait()

    @pl.when(first)
    def _():
        arrived(g2.at[pl.ds(SPAN, SPAN)], SEQ)

    @pl.when(jnp.logical_not(first))
    def _():
        arrived(x2.at[pl.ds(SPAN, SPAN)], SEQ)

    def onward(j, carry):
        cols = pl.ds(pl.multiple_of(j * 256, 256), 256)
        prod[0, :, cols] = jnp.dot(toe[0], x2[:, cols], preferred_element_type=F32)
        grad = g2[:SPAN, cols].astype(F32)
        for k in range(NODES):
            inn[k : k + 1, cols] = jnp.sum(
                prod[0, k * SPAN : (k + 1) * SPAN, cols] * grad, axis=0, keepdims=True
            )
        return carry

    lax.fori_loop(0, 4, onward, 0)
    wide = BLOCKS // 2 * SPAN
    mine = pl.ds(pl.multiple_of(core * wide, wide), wide)
    other = pl.ds(pl.multiple_of((1 - core) * wide, wide), wide)
    half = push_to(inn.at[:, other], half_rcv, HALF, sibling)
    half.start()
    arrived(half_rcv, HALF)
    inner = inn[:, mine] + half_rcv[...]
    for b in range(BLOCKS // 2):
        inn_send[b] = inner[:, b * SPAN : (b + 1) * SPAN].astype(BF16)
    inner_args = [
        (inn_send.at[b], inn_rcv.at[chip], INN, scanner_of(core * (BLOCKS // 2) + b, 0))
        for b in range(BLOCKS // 2)
    ]
    for args in inner_args:
        send(*args)

    def back(j, carry):
        cols = pl.ds(pl.multiple_of(j * 256, 256), 256)
        prod[1, :, cols] = jnp.dot(toe[1], g2[:, cols], preferred_element_type=F32)
        return carry

    lax.fori_loop(0, 4, back, 0)

    def chunk_at(i):
        return i + core * (CHUNKS - 1 - 2 * i)

    def by_z(n):
        return lax.rem(n, 2) * 16 + lax.div(n, 2)

    @pl.when(scans)
    def _():
        arrived(prm_rcv, PRM)
        lane8 = lax.broadcasted_iota(jnp.int32, (8, SPAN), 1)
        row8 = lax.broadcasted_iota(jnp.int32, (8, SPAN), 0)
        halves = []
        for r in range(4):
            packed = jnp.concatenate([prm_rcv[k, r : r + 1, :] for k in range(8)], axis=0)
            skewed = pltpu.roll(packed, 0, 1, stride=16, stride_axis=0)
            out = jnp.zeros((8, SPAN), F32)
            for j in range(8):
                turned = pltpu.roll(skewed, (SPAN - 16 * j) % SPAN, 1)
                turned = jnp.where(lane8 // 16 == row8, turned, 0.0)
                out = jnp.where(row8 == j, jnp.sum(turned, axis=0, keepdims=True), out)
            halves.append(out)
        decay = jnp.concatenate(halves[:2], axis=0)
        residue = jnp.concatenate(halves[2:], axis=0)
        scale = jnp.sqrt(falling(2.0 * decay))
        gain = residue * scale
        keep = 1.0 - falling(decay)
        points = nodes()
        for k in range(NODES):
            psi[k] = jnp.exp(decay * float(-points[k]))
        where = jnp.zeros((NODES, SPAN), F32)
        rows = lax.broadcasted_iota(jnp.int32, (NODES, SPAN), 0)
        for k in range(NODES):
            where = jnp.where(rows == k, float(-points[k]), where)
        kappa = jnp.zeros((NODES, SPAN), F32)
        for m in range(MODES):
            wave = jnp.exp(where * decay[m : m + 1, :]) * gain[m : m + 1, :]
            kappa = kappa + wave
            push[m] = wave * keep[m : m + 1, :]
        kap_send[...] = kappa.astype(BF16)
        scalers[0], scalers[1] = scale, keep

        pl.semaphore_wait(barrier, DEVICES - 2 * BLOCKS)

        def tell(n, carry):
            @pl.when(jnp.logical_or(lax.div(n, 2) < NEAR, lax.rem(lax.div(n, 2), 2) == core))
            def _():
                send(kap_send, kap_rcv.at[block], KAP, 2 * by_z(n) + core)

            return carry

        lax.fori_loop(0, CHUNKS, tell, 0)

        arrived(mom_rcv, MOM)

        def expand(b, carry):
            mu = mom_rcv[b].astype(F32)
            total = psi[0] * mu[0:1, :]
            for k in range(1, NODES):
                total = total + psi[k] * mu[k : k + 1, :]
            ebuf[b] = total
            return carry

        lax.fori_loop(0, CHUNKS, expand, 0, unroll=4)

        @pl.when(core == 1)
        def _():
            push_to(ebuf, sib_rcv, SIB, me - 1).start()

        far = jnp.exp(decay * float(-PAIR))

        def step(i, state):
            b = chunk_at(i)
            before[b] = state
            total = push[0] * state[0:1, :]
            for m in range(1, MODES):
                total = total + push[m] * state[m : m + 1, :]
            ent_send[b] = total.astype(BF16)
            return state * far + ebuf[b]

        lax.fori_loop(0, CHUNKS, step, jnp.zeros((MODES, SPAN), F32), unroll=4)

        def tell_entering(n, carry):
            b = by_z(n)
            send(ent_send.at[b], ent_rcv.at[core, block], ENT, 2 * b + core)

            @pl.when(lax.div(n, 2) < NEAR)
            def _():
                send(ent_send.at[b], ent_rcv.at[core, block], ENT, 2 * b + 1 - core)

            return carry

        lax.fori_loop(0, CHUNKS, tell_entering, 0)

    arrived(kap_rcv, KAP)
    passes_taps = jnp.logical_and(z >= NEAR, lax.rem(z, 2) == core)

    @pl.when(passes_taps)
    def _():
        push_to(kap_rcv, kap_rcv, KAP, sibling).start()

    def gather(b, carry):
        cols = pl.ds(pl.multiple_of(b * SPAN, SPAN), SPAN)
        kappa = kap_rcv[b].astype(F32)
        for c, acc in ((0, y_acc), (1, r_acc)):
            total = prod[c, :SPAN, cols] * kappa[0:1, :]
            for k in range(1, NODES):
                total = total + prod[c, k * SPAN : (k + 1) * SPAN, cols] * kappa[k : k + 1, :]
            acc[:, cols] = total
        return carry

    lax.fori_loop(0, BLOCKS, gather, 0)
    @pl.when(jnp.logical_and(scans, first))
    def _():
        scale, keep = scalers[0], scalers[1]
        arrived(sib_rcv, SIB)
        arrived(inn_rcv, INN)

        def cross(b, carry):
            total, inner = carry
            return total + before[b] * sib_rcv[b], inner + inn_rcv[b].astype(F32)

        zero = jnp.zeros((MODES, SPAN), F32)
        total, inner = lax.fori_loop(0, CHUNKS, cross, (zero, zero), unroll=4)
        total = total * keep
        for k in range(NODES):
            total = total + psi[k] * inner[k : k + 1, :]
        sco_send[...] = total * scale * (1.0 / math.sqrt(SPAN * DEVICES))
        for k in range(8):
            send(sco_send, sco_rcv, SCO, 8 * block + k)

    for args in moment_args + inner_args + param_args:
        sent(*args)
    part.wait_send()
    half.wait_send()

    @pl.when(passes_taps)
    def _():
        push_to(kap_rcv, kap_rcv, KAP, sibling).wait_send()

    @pl.when(first)
    def _():
        push_to(x2.at[pl.ds(0, SPAN)], x2.at[pl.ds(SPAN, SPAN)], SEQ, sibling).wait_send()

    @pl.when(jnp.logical_not(first))
    def _():
        push_to(g2.at[pl.ds(0, SPAN)], g2.at[pl.ds(SPAN, SPAN)], SEQ, sibling).wait_send()

    @pl.when(scans)
    def _():
        def told(n, carry):
            @pl.when(jnp.logical_or(lax.div(n, 2) < NEAR, lax.rem(lax.div(n, 2), 2) == core))
            def _():
                sent(kap_send, kap_rcv.at[block], KAP, 2 * by_z(n) + core)

            return carry

        lax.fori_loop(0, CHUNKS, told, 0)

        def stepped(n, carry):
            b = by_z(n)
            sent(ent_send.at[b], ent_rcv.at[core, block], ENT, 2 * b + core)

            @pl.when(lax.div(n, 2) < NEAR)
            def _():
                sent(ent_send.at[b], ent_rcv.at[core, block], ENT, 2 * b + 1 - core)

            return carry

        lax.fori_loop(0, CHUNKS, stepped, 0)

        @pl.when(core == 1)
        def _():
            push_to(ebuf, sib_rcv, SIB, me - 1).wait_send()

    near = z < NEAR

    @pl.when(near)
    def _():
        arrived(ent_rcv, ENT)

    def relay():
        return push_to(ent_rcv.at[core], ent_rcv.at[core], RLY, sibling)

    @pl.when(jnp.logical_not(near))
    def _():
        arrived(ent_rcv.at[core], ENT)
        relay().start()
        arrived(ent_rcv.at[1 - core], RLY)

    for b in range(BLOCKS):
        cols = slice(b * SPAN, (b + 1) * SPAN)
        for c, acc, out in ((0, y_acc, y_out), (1, r_acc, r_out)):
            entering = ent_rcv[c, b]
            both = jnp.concatenate([entering, entering], axis=0)
            total = acc[:, cols] + jnp.dot(spr[2 * core + c], both, preferred_element_type=F32)
            out[:, cols] = total.astype(BF16)

    arrived(sco_rcv, SCO)
    turned = pltpu.roll(sco_rcv[...], lax.rem(SPAN - 16 * own_part, SPAN), 1)
    s_out[...] = jnp.transpose(turned)[:OWN, :]

    @pl.when(z >= NEAR)
    def _():
        relay().wait_send()

    @pl.when(jnp.logical_and(scans, first))
    def _():
        for k in range(8):
            sent(sco_send, sco_rcv, SCO, 8 * block + k)


def last_products(
    y_ref, r_ref, go_ref, v_ref, k_ref, score_ref, gq_out, gk_out, gv_out, score_out, gq, gk, gv, score, sem
):
    score[...] = score_ref[...]
    copies = [pltpu.make_async_copy(score, score_out, sem.at[0])]
    copies[0].start()
    rows = 32
    for n in range(SPAN // rows):
        part = pl.ds(n * rows, rows)
        y = y_ref[part, :].astype(F32)
        r = r_ref[part, :].astype(F32)
        for c, (mine, gate, left, out) in enumerate(
            ((gq, go_ref, y, gq_out), (gk, v_ref, r, gk_out), (gv, k_ref, r, gv_out))
        ):
            mine[part, :] = (left * gate[part, :].astype(F32)).astype(BF16)
            copy = pltpu.make_async_copy(mine.at[part], out.at[part], sem.at[1 + 3 * n + c])
            copy.start()
            copies.append(copy)
    for copy in copies:
        copy.wait()


def body(query_gate, key_gate, value_input, grad_out, residues, decay):
    toeplitz, moments, spread = (jnp.asarray(t) for t in tables())
    tokens, channels = query_gate.shape
    vm = pltpu.VMEM
    gate = vm((tokens, channels), BF16)
    scratch = [
        gate, gate, gate, gate, vm((OWN, MODES), F32), vm((OWN, MODES), F32),
        vm(toeplitz.shape, BF16), vm(moments.shape, BF16), vm(spread.shape, BF16),
        vm((PAIR, channels), BF16), vm((PAIR, channels), BF16),
        vm((2, NODES * SPAN, channels), F32), vm((NODES, channels), F32),
        vm((tokens, channels), F32), vm((tokens, channels), F32),
        vm((NODES, channels), F32), vm((NODES, channels), F32), vm((NODES, channels // 2), F32),
        vm((BLOCKS, NODES, SPAN), BF16), vm((BLOCKS // 2, NODES, SPAN), BF16), vm((4, SPAN), F32),
        vm((CHUNKS, NODES, SPAN), BF16), vm((CHUNKS, NODES, SPAN), BF16), vm((8, 4, SPAN), F32),
        vm((BLOCKS, NODES, SPAN), BF16), vm((2, BLOCKS, NODES, SPAN), BF16), vm((MODES, SPAN), F32),
        vm((CHUNKS, MODES, SPAN), F32),
        vm((NODES, MODES, SPAN), F32), vm((MODES, NODES, SPAN), F32), vm((CHUNKS, MODES, SPAN), F32),
        vm((CHUNKS, MODES, SPAN), F32), vm((CHUNKS, NODES, SPAN), BF16), vm((NODES, SPAN), BF16),
        vm((MODES, SPAN), F32), vm((2, MODES, SPAN), F32),
        pltpu.SemaphoreType.DMA((9,)), pltpu.SemaphoreType.DMA((11,)), pltpu.SemaphoreType.DMA((11,)),
    ]
    hbm = pl.BlockSpec(memory_space=pltpu.HBM)
    vmem = pl.BlockSpec(memory_space=pltpu.VMEM)
    output, backward, score = pl.pallas_call(
        kernel,
        out_shape=(
            jax.ShapeDtypeStruct((tokens, channels), BF16),
            jax.ShapeDtypeStruct((tokens, channels), BF16),
            jax.ShapeDtypeStruct((OWN, MODES), F32),
        ),
        in_specs=[hbm] * 9,
        out_specs=(vmem, vmem, vmem),
        scratch_shapes=scratch,
        compiler_params=pltpu.CompilerParams(
            collective_id=0, has_side_effects=True, vmem_limit_bytes=48 * 2**20
        ),
        cost_estimate=pl.CostEstimate(flops=2**31, bytes_accessed=2**22, transcendentals=0),
        name="chunk_convolution",
    )(*(pltpu.with_memory_space_constraint(a, pltpu.HBM) for a in (
        query_gate, key_gate, value_input, grad_out, residues, decay, toeplitz, moments, spread)))
    wide = jax.ShapeDtypeStruct((tokens, channels), BF16)
    return pl.pallas_call(
        last_products,
        out_shape=(wide, wide, wide, jax.ShapeDtypeStruct((OWN, MODES), F32)),
        in_specs=[vmem] * 6,
        out_specs=(pl.BlockSpec(memory_space=pl.ANY),) * 4,
        scratch_shapes=[gate, gate, gate, vm((OWN, MODES), F32), pltpu.SemaphoreType.DMA((13,))],
        compiler_params=pltpu.CompilerParams(vmem_limit_bytes=8 * 2**20),
        name="last_products",
    )(output, backward, grad_out, value_input, key_gate, score)


def solution(mesh):
    gate = P("seq", "chan")
    rows = P(("chan", "seq"), None)
    return jax.shard_map(
        body,
        mesh=mesh,
        in_specs=(gate, gate, gate, gate, rows, rows),
        out_specs=(gate, gate, gate, rows),
        check_vma=False,
    )
```

```python
import functools
import math

import jax
import jax.numpy as jnp
import ml_dtypes
import numpy as np
from jax import lax
from jax.experimental import pallas as pl
from jax.experimental.pallas import tpu as pltpu
from jax.sharding import PartitionSpec as P

MESH = pl.DeviceIdType.MESH
F32 = jnp.float32
BF16 = jnp.bfloat16
SPAN = 128
PAIR = 2 * SPAN
NODES = 16
MODES = 16
BLOCKS = 8
DEVICES = 64
CHUNKS = 32
OWN = 16
BEND = 200.0
Z_FIRST, Z_STEP = 0, 1
NEAR = 2
MOM, INN, PRM, KAP, ENT, SCO, SIB, PART, SEQ, RLY, HALF = range(11)


def scan_device(block, core):
    z = (Z_FIRST + Z_STEP * (block % 4)) % 16
    return (block // 4) * 32 + z * 2 + core


def bent(lag):
    return lag / (lag + BEND)


def bent_nodes():
    k = np.arange(NODES)
    half = bent(PAIR - 1.0) / 2.0
    return half + half * np.cos(np.pi * (2 * k + 1) / (2 * NODES))


def nodes():
    u = bent_nodes()
    return BEND * u / (1.0 - u)


def cardinal():
    u = bent_nodes()
    at = bent(np.arange(PAIR, dtype=np.float64))
    out = np.ones((NODES, PAIR))
    for k in range(NODES):
        for j in range(NODES):
            if j != k:
                out[k] *= (at - u[j]) / (u[k] - u[j])
    return out


def split(a, axis):
    high = a.astype(ml_dtypes.bfloat16)
    low = (a - high.astype(np.float64)).astype(ml_dtypes.bfloat16)
    return np.concatenate([high, low], axis=axis)


@functools.cache
def tables():
    phi = cardinal()
    t = np.arange(SPAN)
    lag = t[:, None] - t[None, :]
    inside = lag >= 0
    own = np.where(inside[None], phi[:, np.where(inside, lag, 0)], 0.0)
    cross = phi[:, lag + SPAN]
    toeplitz = np.stack([np.concatenate([a, b], axis=-1) for a, b in (
        (own, cross), (own.transpose(0, 2, 1), cross.transpose(0, 2, 1)))])
    toeplitz = toeplitz.reshape(2, NODES * SPAN, PAIR).astype(ml_dtypes.bfloat16)
    ahead, behind = phi[:, :SPAN], phi[:, SPAN:]
    moments = np.stack([np.stack([split(a, 0) for a in pair]) for pair in (
        (behind[:, ::-1], ahead), (ahead[:, ::-1], behind))])
    spread = np.stack([np.stack([split(a.T, 1) for a in pair]) for pair in (
        (ahead, behind[:, ::-1]), (behind, ahead[:, ::-1]))])
    return toeplitz, moments.reshape(4, 2 * NODES, SPAN), spread.reshape(4, SPAN, 2 * NODES)


def falling(u):
    total = jnp.full_like(u, -1.0 / 5040.0)
    for c in (720.0, -120.0, 24.0, -6.0, 2.0, -1.0):
        total = total * u - 1.0 / c
    return total * u


def kernel(
    q_hbm, k_hbm, v_hbm, go_hbm, res_hbm, dec_hbm, toe_hbm, mom_hbm, spr_hbm,
    y_out, r_out, s_out,
    q_in, k_in, v_in, go_in, res_in, dec_in, toe, mom, spr,
    x2, g2, prod, inn, y_acc, r_acc,
    part_send, part_rcv, half_rcv,
    mom_send, inn_send, prm_send,
    mom_rcv, inn_rcv, prm_rcv, kap_rcv, ent_rcv, sco_rcv, sib_rcv,
    psi, push, ebuf, before, ent_send, kap_send, sco_send, scalers,
    in_sem, send_sem, recv_sem,
):
    me = lax.axis_index("seq")
    core = lax.rem(me, 2)
    chip = lax.div(me, 2)
    sibling = me + 1 - 2 * core
    z = lax.rem(chip, 16)
    y_hi = lax.div(me, 32)
    ahead = lax.rem(z - Z_FIRST + 16, 16)
    scans = jnp.logical_and(lax.rem(ahead, Z_STEP) == 0, ahead < 4 * Z_STEP)
    block = y_hi * 4 + lax.rem(lax.div(ahead, Z_STEP), 4)
    own_block, own_part = lax.div(me, 8), lax.rem(me, 8)

    def scanner_of(b, c):
        return lax.div(b, 4) * 32 + lax.rem(Z_FIRST + Z_STEP * lax.rem(b, 4), 16) * 2 + c

    loads = [
        pltpu.make_async_copy(src, dst, in_sem.at[n])
        for n, (src, dst) in enumerate(
            [
                (res_hbm, res_in), (dec_hbm, dec_in),
                (k_hbm, k_in), (v_hbm, v_in), (go_hbm, go_in), (q_hbm, q_in), (mom_hbm, mom), (spr_hbm, spr), (toe_hbm, toe),
            ]
        )
    ]
    for load in loads:
        load.start()

    barrier = pltpu.get_barrier_semaphore()

    def greet(device):
        pl.semaphore_signal(barrier, inc=1, device_id={"seq": device}, device_id_type=MESH)

    @pl.when(scans)
    def _():
        for b in range(BLOCKS):
            for c in range(2):
                device = scan_device(b, c)

                @pl.when(me != device)
                def _():
                    greet(device)

        def one(n, carry):
            z_there = lax.rem(Z_FIRST + 4 + lax.rem(lax.div(n, 4) + 4, 12), 16)
            greet(lax.rem(n, 4) // 2 * 32 + z_there * 2 + lax.rem(n, 2))
            return carry

        lax.fori_loop(0, DEVICES - 2 * BLOCKS, one, 0)
        pl.semaphore_wait(barrier, 2 * BLOCKS - 1)

    @pl.when(jnp.logical_not(scans))
    def _():
        greet(sibling)

    def push_to(src, dst, kind, device):
        return pltpu.make_async_remote_copy(
            src_ref=src, dst_ref=dst, send_sem=send_sem.at[kind], recv_sem=recv_sem.at[kind],
            device_id={"seq": device}, device_id_type=MESH,
        )

    def send(src, dst, kind, device):
        @pl.when(me != device)
        def _():
            push_to(src, dst, kind, device).start()

        @pl.when(me == device)
        def _():
            pltpu.make_async_copy(src, dst, recv_sem.at[kind]).start()

    def sent(src, dst, kind, device):
        @pl.when(me != device)
        def _():
            push_to(src, dst, kind, device).wait_send()

    def arrived(ref, kind):
        pltpu.make_async_copy(ref, ref, recv_sem.at[kind]).wait()

    loads[0].wait()
    loads[1].wait()
    lane16 = lax.broadcasted_iota(jnp.int32, (OWN, SPAN), 1)
    row16 = lax.broadcasted_iota(jnp.int32, (OWN, SPAN), 0)
    for n, ref in ((0, dec_in), (1, res_in)):
        value = ref[...]
        for r in range(2):
            wide = jnp.zeros((OWN, SPAN), F32)
            for j in range(8):
                column = jnp.broadcast_to(value[:, 8 * r + j : 8 * r + j + 1], (OWN, SPAN))
                wide = jnp.where(lane16 // 16 == j, column, wide)
            wide = jnp.where(lane16 % 16 == row16, wide, 0.0)
            prm_send[2 * n + r : 2 * n + r + 1, :] = jnp.sum(wide, axis=0, keepdims=True)

    for n in (2, 3, 4, 5, 6):
        loads[n].wait()
    x = (k_in[...].astype(F32) * v_in[...].astype(F32)).astype(BF16)
    g = (go_in[...].astype(F32) * q_in[...].astype(F32)).astype(BF16)
    first = core == 0

    def moment(c, value):
        both = jnp.dot(mom[2 * core + c], value, preferred_element_type=F32)
        return both[:NODES] + both[NODES:]

    part_send[...] = moment(1 - core, jnp.where(first, g, x))

    @pl.when(jnp.logical_not(scans))
    def _():
        pl.semaphore_wait(barrier, 2 * BLOCKS + 1)

    param_args = [(prm_send, prm_rcv.at[own_part], PRM, scanner_of(own_block, c)) for c in range(2)]
    for args in param_args:
        send(*args)

    part = push_to(part_send, part_rcv, PART, sibling)
    part.start()
    kept = moment(core, jnp.where(first, x, g))
    x2[:SPAN, :] = x
    g2[:SPAN, :] = g

    @pl.when(first)
    def _():
        push_to(x2.at[pl.ds(0, SPAN)], x2.at[pl.ds(SPAN, SPAN)], SEQ, sibling).start()
        x2[SPAN:, :] = jnp.zeros((SPAN, x2.shape[1]), BF16)

    @pl.when(jnp.logical_not(first))
    def _():
        push_to(g2.at[pl.ds(0, SPAN)], g2.at[pl.ds(SPAN, SPAN)], SEQ, sibling).start()
        g2[SPAN:, :] = jnp.zeros((SPAN, g2.shape[1]), BF16)

    arrived(part_rcv, PART)
    total = (kept + part_rcv[...]).astype(BF16)
    for b in range(BLOCKS):
        mom_send[b] = total[:, b * SPAN : (b + 1) * SPAN]
    moment_args = [(mom_send.at[b], mom_rcv.at[chip], MOM, scan_device(b, 0) + core) for b in range(BLOCKS)]
    for args in moment_args:
        send(*args)

    @pl.when(jnp.logical_not(scans))
    def _():
        for b in range(BLOCKS):
            for c in range(2):
                greet(scan_device(b, c))


    loads[7].wait()
    loads[8].wait()

    @pl.when(first)
    def _():
        arrived(g2.at[pl.ds(SPAN, SPAN)], SEQ)

    @pl.when(jnp.logical_not(first))
    def _():
        arrived(x2.at[pl.ds(SPAN, SPAN)], SEQ)

    def onward(j, carry):
        cols = pl.ds(pl.multiple_of(j * 256, 256), 256)
        prod[0, :, cols] = jnp.dot(toe[0], x2[:, cols], preferred_element_type=F32)
        grad = g2[:SPAN, cols].astype(F32)
        for k in range(NODES):
            inn[k : k + 1, cols] = jnp.sum(
                prod[0, k * SPAN : (k + 1) * SPAN, cols] * grad, axis=0, keepdims=True
            )
        return carry

    lax.fori_loop(0, 4, onward, 0)
    wide = BLOCKS // 2 * SPAN
    mine = pl.ds(pl.multiple_of(core * wide, wide), wide)
    other = pl.ds(pl.multiple_of((1 - core) * wide, wide), wide)
    half = push_to(inn.at[:, other], half_rcv, HALF, sibling)
    half.start()
    arrived(half_rcv, HALF)
    inner = inn[:, mine] + half_rcv[...]
    for b in range(BLOCKS // 2):
        inn_send[b] = inner[:, b * SPAN : (b + 1) * SPAN].astype(BF16)
    inner_args = [
        (inn_send.at[b], inn_rcv.at[chip], INN, scanner_of(core * (BLOCKS // 2) + b, 0))
        for b in range(BLOCKS // 2)
    ]
    for args in inner_args:
        send(*args)

    def back(j, carry):
        cols = pl.ds(pl.multiple_of(j * 256, 256), 256)
        prod[1, :, cols] = jnp.dot(toe[1], g2[:, cols], preferred_element_type=F32)
        return carry

    lax.fori_loop(0, 4, back, 0)

    def chunk_at(i):
        return i + core * (CHUNKS - 1 - 2 * i)

    def by_z(n):
        return lax.rem(n + 1 + y_hi, 2) * 16 + lax.div(n, 2)

    @pl.when(scans)
    def _():
        arrived(prm_rcv, PRM)
        lane8 = lax.broadcasted_iota(jnp.int32, (8, SPAN), 1)
        row8 = lax.broadcasted_iota(jnp.int32, (8, SPAN), 0)
        halves = []
        for r in range(4):
            packed = jnp.concatenate([prm_rcv[k, r : r + 1, :] for k in range(8)], axis=0)
            skewed = pltpu.roll(packed, 0, 1, stride=16, stride_axis=0)
            out = jnp.zeros((8, SPAN), F32)
            for j in range(8):
                turned = pltpu.roll(skewed, (SPAN - 16 * j) % SPAN, 1)
                turned = jnp.where(lane8 // 16 == row8, turned, 0.0)
                out = jnp.where(row8 == j, jnp.sum(turned, axis=0, keepdims=True), out)
            halves.append(out)
        decay = jnp.concatenate(halves[:2], axis=0)
        residue = jnp.concatenate(halves[2:], axis=0)
        scale = jnp.sqrt(falling(2.0 * decay))
        gain = residue * scale
        keep = 1.0 - falling(decay)
        points = nodes()
        for k in range(NODES):
            psi[k] = jnp.exp(decay * float(-points[k]))
        where = jnp.zeros((NODES, SPAN), F32)
        rows = lax.broadcasted_iota(jnp.int32, (NODES, SPAN), 0)
        for k in range(NODES):
            where = jnp.where(rows == k, float(-points[k]), where)
        kappa = jnp.zeros((NODES, SPAN), F32)
        for m in range(MODES):
            wave = jnp.exp(where * decay[m : m + 1, :]) * gain[m : m + 1, :]
            kappa = kappa + wave
            push[m] = wave * keep[m : m + 1, :]
        kap_send[...] = kappa.astype(BF16)
        scalers[0], scalers[1] = scale, keep

        pl.semaphore_wait(barrier, DEVICES - 2 * BLOCKS)

        def tell(n, carry):
            @pl.when(jnp.logical_or(lax.div(n, 2) < NEAR, lax.rem(lax.div(n, 2), 2) == core))
            def _():
                send(kap_send, kap_rcv.at[block], KAP, 2 * by_z(n) + core)

            return carry

        lax.fori_loop(0, CHUNKS, tell, 0)

        arrived(mom_rcv, MOM)

        def expand(b, carry):
            mu = mom_rcv[b].astype(F32)
            total = psi[0] * mu[0:1, :]
            for k in range(1, NODES):
                total = total + psi[k] * mu[k : k + 1, :]
            ebuf[b] = total
            return carry

        lax.fori_loop(0, CHUNKS, expand, 0, unroll=4)

        @pl.when(core == 1)
        def _():
            push_to(ebuf, sib_rcv, SIB, me - 1).start()

        far = jnp.exp(decay * float(-PAIR))

        def step(i, state):
            b = chunk_at(i)
            before[b] = state
            total = push[0] * state[0:1, :]
            for m in range(1, MODES):
                total = total + push[m] * state[m : m + 1, :]
            ent_send[b] = total.astype(BF16)
            return state * far + ebuf[b]

        lax.fori_loop(0, CHUNKS, step, jnp.zeros((MODES, SPAN), F32), unroll=4)

        def tell_entering(n, carry):
            b = by_z(n)
            send(ent_send.at[b], ent_rcv.at[core, block], ENT, 2 * b + core)

            @pl.when(lax.div(n, 2) < NEAR)
            def _():
                send(ent_send.at[b], ent_rcv.at[core, block], ENT, 2 * b + 1 - core)

            return carry

        lax.fori_loop(0, CHUNKS, tell_entering, 0)

    arrived(kap_rcv, KAP)
    passes_taps = jnp.logical_and(z >= NEAR, lax.rem(z, 2) == core)

    @pl.when(passes_taps)
    def _():
        push_to(kap_rcv, kap_rcv, KAP, sibling).start()

    def gather(b, carry):
        cols = pl.ds(pl.multiple_of(b * SPAN, SPAN), SPAN)
        kappa = kap_rcv[b].astype(F32)
        for c, acc in ((0, y_acc), (1, r_acc)):
            total = prod[c, :SPAN, cols] * kappa[0:1, :]
            for k in range(1, NODES):
                total = total + prod[c, k * SPAN : (k + 1) * SPAN, cols] * kappa[k : k + 1, :]
            acc[:, cols] = total
        return carry

    lax.fori_loop(0, BLOCKS, gather, 0)
    @pl.when(jnp.logical_and(scans, first))
    def _():
        scale, keep = scalers[0], scalers[1]
        arrived(sib_rcv, SIB)
        arrived(inn_rcv, INN)

        def cross(b, carry):
            total, inner = carry
            return total + before[b] * sib_rcv[b], inner + inn_rcv[b].astype(F32)

        zero = jnp.zeros((MODES, SPAN), F32)
        total, inner = lax.fori_loop(0, CHUNKS, cross, (zero, zero), unroll=4)
        total = total * keep
        for k in range(NODES):
            total = total + psi[k] * inner[k : k + 1, :]
        sco_send[...] = total * scale * (1.0 / math.sqrt(SPAN * DEVICES))
        for k in range(8):
            send(sco_send, sco_rcv, SCO, 8 * block + k)

    for args in moment_args + inner_args + param_args:
        sent(*args)
    part.wait_send()
    half.wait_send()

    @pl.when(passes_taps)
    def _():
        push_to(kap_rcv, kap_rcv, KAP, sibling).wait_send()

    @pl.when(first)
    def _():
        push_to(x2.at[pl.ds(0, SPAN)], x2.at[pl.ds(SPAN, SPAN)], SEQ, sibling).wait_send()

    @pl.when(jnp.logical_not(first))
    def _():
        push_to(g2.at[pl.ds(0, SPAN)], g2.at[pl.ds(SPAN, SPAN)], SEQ, sibling).wait_send()

    @pl.when(scans)
    def _():
        def told(n, carry):
            @pl.when(jnp.logical_or(lax.div(n, 2) < NEAR, lax.rem(lax.div(n, 2), 2) == core))
            def _():
                sent(kap_send, kap_rcv.at[block], KAP, 2 * by_z(n) + core)

            return carry

        lax.fori_loop(0, CHUNKS, told, 0)

        def stepped(n, carry):
            b = by_z(n)
            sent(ent_send.at[b], ent_rcv.at[core, block], ENT, 2 * b + core)

            @pl.when(lax.div(n, 2) < NEAR)
            def _():
                sent(ent_send.at[b], ent_rcv.at[core, block], ENT, 2 * b + 1 - core)

            return carry

        lax.fori_loop(0, CHUNKS, stepped, 0)

        @pl.when(core == 1)
        def _():
            push_to(ebuf, sib_rcv, SIB, me - 1).wait_send()

    near = z < NEAR

    @pl.when(near)
    def _():
        arrived(ent_rcv, ENT)

    def relay():
        return push_to(ent_rcv.at[core], ent_rcv.at[core], RLY, sibling)

    @pl.when(jnp.logical_not(near))
    def _():
        arrived(ent_rcv.at[core], ENT)
        relay().start()
        arrived(ent_rcv.at[1 - core], RLY)

    for b in range(BLOCKS):
        cols = slice(b * SPAN, (b + 1) * SPAN)
        for c, acc, out in ((0, y_acc, y_out), (1, r_acc, r_out)):
            entering = ent_rcv[c, b]
            both = jnp.concatenate([entering, entering], axis=0)
            total = acc[:, cols] + jnp.dot(spr[2 * core + c], both, preferred_element_type=F32)
            out[:, cols] = total.astype(BF16)

    arrived(sco_rcv, SCO)
    turned = pltpu.roll(sco_rcv[...], lax.rem(SPAN - 16 * own_part, SPAN), 1)
    s_out[...] = jnp.transpose(turned)[:OWN, :]

    @pl.when(z >= NEAR)
    def _():
        relay().wait_send()

    @pl.when(jnp.logical_and(scans, first))
    def _():
        for k in range(8):
            sent(sco_send, sco_rcv, SCO, 8 * block + k)


def last_products(
    y_ref, r_ref, go_ref, v_ref, k_ref, score_ref, gq_out, gk_out, gv_out, score_out, gq, gk, gv, score, sem
):
    score[...] = score_ref[...]
    copies = [pltpu.make_async_copy(score, score_out, sem.at[0])]
    copies[0].start()
    rows = 32
    for n in range(SPAN // rows):
        part = pl.ds(n * rows, rows)
        y = y_ref[part, :].astype(F32)
        r = r_ref[part, :].astype(F32)
        for c, (mine, gate, left, out) in enumerate(
            ((gq, go_ref, y, gq_out), (gk, v_ref, r, gk_out), (gv, k_ref, r, gv_out))
        ):
            mine[part, :] = (left * gate[part, :].astype(F32)).astype(BF16)
            copy = pltpu.make_async_copy(mine.at[part], out.at[part], sem.at[1 + 3 * n + c])
            copy.start()
            copies.append(copy)
    for copy in copies:
        copy.wait()


def body(query_gate, key_gate, value_input, grad_out, residues, decay):
    toeplitz, moments, spread = (jnp.asarray(t) for t in tables())
    tokens, channels = query_gate.shape
    vm = pltpu.VMEM
    gate = vm((tokens, channels), BF16)
    scratch = [
        gate, gate, gate, gate, vm((OWN, MODES), F32), vm((OWN, MODES), F32),
        vm(toeplitz.shape, BF16), vm(moments.shape, BF16), vm(spread.shape, BF16),
        vm((PAIR, channels), BF16), vm((PAIR, channels), BF16),
        vm((2, NODES * SPAN, channels), F32), vm((NODES, channels), F32),
        vm((tokens, channels), F32), vm((tokens, channels), F32),
        vm((NODES, channels), F32), vm((NODES, channels), F32), vm((NODES, channels // 2), F32),
        vm((BLOCKS, NODES, SPAN), BF16), vm((BLOCKS // 2, NODES, SPAN), BF16), vm((4, SPAN), F32),
        vm((CHUNKS, NODES, SPAN), BF16), vm((CHUNKS, NODES, SPAN), BF16), vm((8, 4, SPAN), F32),
        vm((BLOCKS, NODES, SPAN), BF16), vm((2, BLOCKS, NODES, SPAN), BF16), vm((MODES, SPAN), F32),
        vm((CHUNKS, MODES, SPAN), F32),
        vm((NODES, MODES, SPAN), F32), vm((MODES, NODES, SPAN), F32), vm((CHUNKS, MODES, SPAN), F32),
        vm((CHUNKS, MODES, SPAN), F32), vm((CHUNKS, NODES, SPAN), BF16), vm((NODES, SPAN), BF16),
        vm((MODES, SPAN), F32), vm((2, MODES, SPAN), F32),
        pltpu.SemaphoreType.DMA((9,)), pltpu.SemaphoreType.DMA((11,)), pltpu.SemaphoreType.DMA((11,)),
    ]
    hbm = pl.BlockSpec(memory_space=pltpu.HBM)
    vmem = pl.BlockSpec(memory_space=pltpu.VMEM)
    output, backward, score = pl.pallas_call(
        kernel,
        out_shape=(
            jax.ShapeDtypeStruct((tokens, channels), BF16),
            jax.ShapeDtypeStruct((tokens, channels), BF16),
            jax.ShapeDtypeStruct((OWN, MODES), F32),
        ),
        in_specs=[hbm] * 9,
        out_specs=(vmem, vmem, vmem),
        scratch_shapes=scratch,
        compiler_params=pltpu.CompilerParams(
            collective_id=0, has_side_effects=True, vmem_limit_bytes=48 * 2**20
        ),
        cost_estimate=pl.CostEstimate(flops=2**31, bytes_accessed=2**22, transcendentals=0),
        name="chunk_convolution",
    )(*(pltpu.with_memory_space_constraint(a, pltpu.HBM) for a in (
        query_gate, key_gate, value_input, grad_out, residues, decay, toeplitz, moments, spread)))
    wide = jax.ShapeDtypeStruct((tokens, channels), BF16)
    return pl.pallas_call(
        last_products,
        out_shape=(wide, wide, wide, jax.ShapeDtypeStruct((OWN, MODES), F32)),
        in_specs=[vmem] * 6,
        out_specs=(pl.BlockSpec(memory_space=pl.ANY),) * 4,
        scratch_shapes=[gate, gate, gate, vm((OWN, MODES), F32), pltpu.SemaphoreType.DMA((13,))],
        compiler_params=pltpu.CompilerParams(vmem_limit_bytes=8 * 2**20),
        name="last_products",
    )(output, backward, grad_out, value_input, key_gate, score)


def solution(mesh):
    gate = P("seq", "chan")
    rows = P(("chan", "seq"), None)
    return jax.shard_map(
        body,
        mesh=mesh,
        in_specs=(gate, gate, gate, gate, rows, rows),
        out_specs=(gate, gate, gate, rows),
        check_vma=False,
    )
```

```python
import functools
import math

import jax
import jax.numpy as jnp
import ml_dtypes
import numpy as np
from jax import lax
from jax.experimental import pallas as pl
from jax.experimental.pallas import tpu as pltpu
from jax.sharding import PartitionSpec as P

MESH = pl.DeviceIdType.MESH
F32 = jnp.float32
BF16 = jnp.bfloat16
SPAN = 128
PAIR = 2 * SPAN
NODES = 16
MODES = 16
BLOCKS = 8
DEVICES = 64
CHUNKS = 32
OWN = 16
BEND = 200.0
Z_FIRST, Z_STEP = 0, 1
NEAR = 2
MOM, INN, PRM, KAP, ENT, SCO, SIB, PART, SEQ, RLY, HALF = range(11)


def scan_device(block, core):
    z = (Z_FIRST + Z_STEP * (block % 4)) % 16
    return (block // 4) * 32 + z * 2 + core


def bent(lag):
    return lag / (lag + BEND)


def bent_nodes():
    k = np.arange(NODES)
    half = bent(PAIR - 1.0) / 2.0
    return half + half * np.cos(np.pi * (2 * k + 1) / (2 * NODES))


def nodes():
    u = bent_nodes()
    return BEND * u / (1.0 - u)


def cardinal():
    u = bent_nodes()
    at = bent(np.arange(PAIR, dtype=np.float64))
    out = np.ones((NODES, PAIR))
    for k in range(NODES):
        for j in range(NODES):
            if j != k:
                out[k] *= (at - u[j]) / (u[k] - u[j])
    return out


def split(a, axis):
    high = a.astype(ml_dtypes.bfloat16)
    low = (a - high.astype(np.float64)).astype(ml_dtypes.bfloat16)
    return np.concatenate([high, low], axis=axis)


@functools.cache
def tables():
    phi = cardinal()
    t = np.arange(SPAN)
    lag = t[:, None] - t[None, :]
    inside = lag >= 0
    own = np.where(inside[None], phi[:, np.where(inside, lag, 0)], 0.0)
    cross = phi[:, lag + SPAN]
    toeplitz = np.stack([np.concatenate([a, b], axis=-1) for a, b in (
        (own, cross), (own.transpose(0, 2, 1), cross.transpose(0, 2, 1)))])
    toeplitz = toeplitz.reshape(2, NODES * SPAN, PAIR).astype(ml_dtypes.bfloat16)
    ahead, behind = phi[:, :SPAN], phi[:, SPAN:]
    moments = np.stack([np.stack([split(a, 0) for a in pair]) for pair in (
        (behind[:, ::-1], ahead), (ahead[:, ::-1], behind))])
    spread = np.stack([np.stack([split(a.T, 1) for a in pair]) for pair in (
        (ahead, behind[:, ::-1]), (behind, ahead[:, ::-1]))])
    return toeplitz, moments.reshape(4, 2 * NODES, SPAN), spread.reshape(4, SPAN, 2 * NODES)


def falling(u):
    total = jnp.full_like(u, -1.0 / 5040.0)
    for c in (720.0, -120.0, 24.0, -6.0, 2.0, -1.0):
        total = total * u - 1.0 / c
    return total * u


def kernel(
    q_hbm, k_hbm, v_hbm, go_hbm, res_hbm, dec_hbm, toe_hbm, mom_hbm, spr_hbm,
    y_out, r_out, s_out,
    q_in, k_in, v_in, go_in, res_in, dec_in, toe, mom, spr,
    x2, g2, prod, inn, y_acc, r_acc,
    part_send, part_rcv, half_rcv,
    mom_send, inn_send, prm_send,
    mom_rcv, inn_rcv, prm_rcv, kap_rcv, ent_rcv, sco_rcv, sib_rcv,
    psi, push, ebuf, before, ent_send, kap_send, sco_send, scalers,
    in_sem, send_sem, recv_sem,
):
    me = lax.axis_index("seq")
    core = lax.rem(me, 2)
    chip = lax.div(me, 2)
    sibling = me + 1 - 2 * core
    z = lax.rem(chip, 16)
    y_hi = lax.div(me, 32)
    ahead = lax.rem(z - Z_FIRST + 16, 16)
    scans = jnp.logical_and(lax.rem(ahead, Z_STEP) == 0, ahead < 4 * Z_STEP)
    block = y_hi * 4 + lax.rem(lax.div(ahead, Z_STEP), 4)
    own_block, own_part = lax.div(me, 8), lax.rem(me, 8)

    def scanner_of(b, c):
        return lax.div(b, 4) * 32 + lax.rem(Z_FIRST + Z_STEP * lax.rem(b, 4), 16) * 2 + c

    loads = [
        pltpu.make_async_copy(src, dst, in_sem.at[n])
        for n, (src, dst) in enumerate(
            [
                (res_hbm, res_in), (dec_hbm, dec_in),
                (k_hbm, k_in), (v_hbm, v_in), (go_hbm, go_in), (q_hbm, q_in), (mom_hbm, mom), (spr_hbm, spr), (toe_hbm, toe),
            ]
        )
    ]
    for load in loads:
        load.start()

    barrier = pltpu.get_barrier_semaphore()

    def greet(device):
        pl.semaphore_signal(barrier, inc=1, device_id={"seq": device}, device_id_type=MESH)

    @pl.when(scans)
    def _():
        for b in range(BLOCKS):
            for c in range(2):
                device = scan_device(b, c)

                @pl.when(me != device)
                def _():
                    greet(device)

        def one(n, carry):
            z_there = lax.rem(Z_FIRST + 4 + lax.rem(lax.div(n, 4) + 4, 12), 16)
            greet(lax.rem(n, 4) // 2 * 32 + z_there * 2 + lax.rem(n, 2))
            return carry

        lax.fori_loop(0, DEVICES - 2 * BLOCKS, one, 0)
        pl.semaphore_wait(barrier, 2 * BLOCKS - 1)

    @pl.when(jnp.logical_not(scans))
    def _():
        greet(sibling)

    def push_to(src, dst, kind, device):
        return pltpu.make_async_remote_copy(
            src_ref=src, dst_ref=dst, send_sem=send_sem.at[kind], recv_sem=recv_sem.at[kind],
            device_id={"seq": device}, device_id_type=MESH,
        )

    def send(src, dst, kind, device):
        @pl.when(me != device)
        def _():
            push_to(src, dst, kind, device).start()

        @pl.when(me == device)
        def _():
            pltpu.make_async_copy(src, dst, recv_sem.at[kind]).start()

    def sent(src, dst, kind, device):
        @pl.when(me != device)
        def _():
            push_to(src, dst, kind, device).wait_send()

    def arrived(ref, kind):
        pltpu.make_async_copy(ref, ref, recv_sem.at[kind]).wait()

    loads[0].wait()
    loads[1].wait()
    lane16 = lax.broadcasted_iota(jnp.int32, (OWN, SPAN), 1)
    row16 = lax.broadcasted_iota(jnp.int32, (OWN, SPAN), 0)
    for n, ref in ((0, dec_in), (1, res_in)):
        value = ref[...]
        for r in range(2):
            wide = jnp.zeros((OWN, SPAN), F32)
            for j in range(8):
                column = jnp.broadcast_to(value[:, 8 * r + j : 8 * r + j + 1], (OWN, SPAN))
                wide = jnp.where(lane16 // 16 == j, column, wide)
            wide = jnp.where(lane16 % 16 == row16, wide, 0.0)
            prm_send[2 * n + r : 2 * n + r + 1, :] = jnp.sum(wide, axis=0, keepdims=True)

    for n in (2, 3, 4, 5, 6):
        loads[n].wait()
    x = (k_in[...].astype(F32) * v_in[...].astype(F32)).astype(BF16)
    g = (go_in[...].astype(F32) * q_in[...].astype(F32)).astype(BF16)
    first = core == 0

    def moment(c, value):
        both = jnp.dot(mom[2 * core + c], value, preferred_element_type=F32)
        return both[:NODES] + both[NODES:]

    part_send[...] = moment(1 - core, jnp.where(first, g, x))

    @pl.when(jnp.logical_not(scans))
    def _():
        pl.semaphore_wait(barrier, 2 * BLOCKS + 1)

    param_args = [(prm_send, prm_rcv.at[own_part], PRM, scanner_of(own_block, c)) for c in range(2)]
    for args in param_args:
        send(*args)

    part = push_to(part_send, part_rcv, PART, sibling)
    part.start()
    kept = moment(core, jnp.where(first, x, g))
    x2[:SPAN, :] = x
    g2[:SPAN, :] = g

    @pl.when(first)
    def _():
        push_to(x2.at[pl.ds(0, SPAN)], x2.at[pl.ds(SPAN, SPAN)], SEQ, sibling).start()
        x2[SPAN:, :] = jnp.zeros((SPAN, x2.shape[1]), BF16)

    @pl.when(jnp.logical_not(first))
    def _():
        push_to(g2.at[pl.ds(0, SPAN)], g2.at[pl.ds(SPAN, SPAN)], SEQ, sibling).start()
        g2[SPAN:, :] = jnp.zeros((SPAN, g2.shape[1]), BF16)

    arrived(part_rcv, PART)
    total = (kept + part_rcv[...]).astype(BF16)
    for b in range(BLOCKS):
        mom_send[b] = total[:, b * SPAN : (b + 1) * SPAN]
    moment_args = [(mom_send.at[b], mom_rcv.at[chip], MOM, scan_device(b, 0) + core) for b in range(BLOCKS)]
    for args in moment_args:
        send(*args)

    @pl.when(jnp.logical_not(scans))
    def _():
        for b in range(BLOCKS):
            for c in range(2):
                greet(scan_device(b, c))


    loads[7].wait()
    loads[8].wait()

    @pl.when(first)
    def _():
        arrived(g2.at[pl.ds(SPAN, SPAN)], SEQ)

    @pl.when(jnp.logical_not(first))
    def _():
        arrived(x2.at[pl.ds(SPAN, SPAN)], SEQ)

    def onward(j, carry):
        cols = pl.ds(pl.multiple_of(j * 256, 256), 256)
        prod[0, :, cols] = jnp.dot(toe[0], x2[:, cols], preferred_element_type=F32)
        grad = g2[:SPAN, cols].astype(F32)
        for k in range(NODES):
            inn[k : k + 1, cols] = jnp.sum(
                prod[0, k * SPAN : (k + 1) * SPAN, cols] * grad, axis=0, keepdims=True
            )
        return carry

    lax.fori_loop(0, 4, onward, 0)
    wide = BLOCKS // 2 * SPAN
    mine = pl.ds(pl.multiple_of(core * wide, wide), wide)
    other = pl.ds(pl.multiple_of((1 - core) * wide, wide), wide)
    half = push_to(inn.at[:, other], half_rcv, HALF, sibling)
    half.start()
    arrived(half_rcv, HALF)
    inner = inn[:, mine] + half_rcv[...]
    for b in range(BLOCKS // 2):
        inn_send[b] = inner[:, b * SPAN : (b + 1) * SPAN].astype(BF16)
    inner_args = [
        (inn_send.at[b], inn_rcv.at[chip], INN, scanner_of(core * (BLOCKS // 2) + b, 0))
        for b in range(BLOCKS // 2)
    ]
    for args in inner_args:
        send(*args)

    def back(j, carry):
        cols = pl.ds(pl.multiple_of(j * 256, 256), 256)
        prod[1, :, cols] = jnp.dot(toe[1], g2[:, cols], preferred_element_type=F32)
        return carry

    lax.fori_loop(0, 4, back, 0)

    def chunk_at(i):
        return i + core * (CHUNKS - 1 - 2 * i)

    def by_z(n):
        return lax.rem(n + 1 + y_hi, 2) * 16 + lax.div(n, 2)

    @pl.when(scans)
    def _():
        arrived(prm_rcv, PRM)
        lane8 = lax.broadcasted_iota(jnp.int32, (8, SPAN), 1)
        row8 = lax.broadcasted_iota(jnp.int32, (8, SPAN), 0)
        halves = []
        for r in range(4):
            packed = jnp.concatenate([prm_rcv[k, r : r + 1, :] for k in range(8)], axis=0)
            skewed = pltpu.roll(packed, 0, 1, stride=16, stride_axis=0)
            out = jnp.zeros((8, SPAN), F32)
            for j in range(8):
                turned = pltpu.roll(skewed, (SPAN - 16 * j) % SPAN, 1)
                turned = jnp.where(lane8 // 16 == row8, turned, 0.0)
                out = jnp.where(row8 == j, jnp.sum(turned, axis=0, keepdims=True), out)
            halves.append(out)
        decay = jnp.concatenate(halves[:2], axis=0)
        residue = jnp.concatenate(halves[2:], axis=0)
        scale = jnp.sqrt(falling(2.0 * decay))
        gain = residue * scale
        keep = 1.0 - falling(decay)
        points = nodes()
        for k in range(NODES):
            psi[k] = jnp.exp(decay * float(-points[k]))
        where = jnp.zeros((NODES, SPAN), F32)
        rows = lax.broadcasted_iota(jnp.int32, (NODES, SPAN), 0)
        for k in range(NODES):
            where = jnp.where(rows == k, float(-points[k]), where)
        kappa = jnp.zeros((NODES, SPAN), F32)
        for m in range(MODES):
            wave = jnp.exp(where * decay[m : m + 1, :]) * gain[m : m + 1, :]
            kappa = kappa + wave
            push[m] = wave * keep[m : m + 1, :]
        kap_send[...] = kappa.astype(BF16)
        scalers[0], scalers[1] = scale, keep

        pl.semaphore_wait(barrier, DEVICES - 2 * BLOCKS)

        def tell(n, carry):
            @pl.when(jnp.logical_or(lax.div(n, 2) < NEAR, lax.rem(lax.div(n, 2), 2) == core))
            def _():
                send(kap_send, kap_rcv.at[block], KAP, 2 * by_z(n) + core)

            return carry

        lax.fori_loop(0, CHUNKS, tell, 0, unroll=4)

        arrived(mom_rcv, MOM)

        def expand(b, carry):
            mu = mom_rcv[b].astype(F32)
            total = psi[0] * mu[0:1, :]
            for k in range(1, NODES):
                total = total + psi[k] * mu[k : k + 1, :]
            ebuf[b] = total
            return carry

        lax.fori_loop(0, CHUNKS, expand, 0, unroll=4)

        @pl.when(core == 1)
        def _():
            push_to(ebuf, sib_rcv, SIB, me - 1).start()

        far = jnp.exp(decay * float(-PAIR))

        def step(i, state):
            b = chunk_at(i)
            before[b] = state
            total = push[0] * state[0:1, :]
            for m in range(1, MODES):
                total = total + push[m] * state[m : m + 1, :]
            ent_send[b] = total.astype(BF16)
            return state * far + ebuf[b]

        lax.fori_loop(0, CHUNKS, step, jnp.zeros((MODES, SPAN), F32), unroll=4)

        def tell_entering(n, carry):
            b = by_z(n)
            send(ent_send.at[b], ent_rcv.at[core, block], ENT, 2 * b + core)

            @pl.when(lax.div(n, 2) < NEAR)
            def _():
                send(ent_send.at[b], ent_rcv.at[core, block], ENT, 2 * b + 1 - core)

            return carry

        lax.fori_loop(0, CHUNKS, tell_entering, 0, unroll=4)

    arrived(kap_rcv, KAP)
    passes_taps = jnp.logical_and(z >= NEAR, lax.rem(z, 2) == core)

    @pl.when(passes_taps)
    def _():
        push_to(kap_rcv, kap_rcv, KAP, sibling).start()

    def gather(b, carry):
        cols = pl.ds(pl.multiple_of(b * SPAN, SPAN), SPAN)
        kappa = kap_rcv[b].astype(F32)
        for c, acc in ((0, y_acc), (1, r_acc)):
            total = prod[c, :SPAN, cols] * kappa[0:1, :]
            for k in range(1, NODES):
                total = total + prod[c, k * SPAN : (k + 1) * SPAN, cols] * kappa[k : k + 1, :]
            acc[:, cols] = total
        return carry

    lax.fori_loop(0, BLOCKS, gather, 0)
    @pl.when(jnp.logical_and(scans, first))
    def _():
        scale, keep = scalers[0], scalers[1]
        arrived(sib_rcv, SIB)
        arrived(inn_rcv, INN)

        def cross(b, carry):
            total, inner = carry
            return total + before[b] * sib_rcv[b], inner + inn_rcv[b].astype(F32)

        zero = jnp.zeros((MODES, SPAN), F32)
        total, inner = lax.fori_loop(0, CHUNKS, cross, (zero, zero), unroll=4)
        total = total * keep
        for k in range(NODES):
            total = total + psi[k] * inner[k : k + 1, :]
        sco_send[...] = total * scale * (1.0 / math.sqrt(SPAN * DEVICES))
        for k in range(8):
            send(sco_send, sco_rcv, SCO, 8 * block + k)

    for args in moment_args + inner_args + param_args:
        sent(*args)
    part.wait_send()
    half.wait_send()

    @pl.when(passes_taps)
    def _():
        push_to(kap_rcv, kap_rcv, KAP, sibling).wait_send()

    @pl.when(first)
    def _():
        push_to(x2.at[pl.ds(0, SPAN)], x2.at[pl.ds(SPAN, SPAN)], SEQ, sibling).wait_send()

    @pl.when(jnp.logical_not(first))
    def _():
        push_to(g2.at[pl.ds(0, SPAN)], g2.at[pl.ds(SPAN, SPAN)], SEQ, sibling).wait_send()

    @pl.when(scans)
    def _():
        def told(n, carry):
            @pl.when(jnp.logical_or(lax.div(n, 2) < NEAR, lax.rem(lax.div(n, 2), 2) == core))
            def _():
                sent(kap_send, kap_rcv.at[block], KAP, 2 * by_z(n) + core)

            return carry

        lax.fori_loop(0, CHUNKS, told, 0)

        def stepped(n, carry):
            b = by_z(n)
            sent(ent_send.at[b], ent_rcv.at[core, block], ENT, 2 * b + core)

            @pl.when(lax.div(n, 2) < NEAR)
            def _():
                sent(ent_send.at[b], ent_rcv.at[core, block], ENT, 2 * b + 1 - core)

            return carry

        lax.fori_loop(0, CHUNKS, stepped, 0)

        @pl.when(core == 1)
        def _():
            push_to(ebuf, sib_rcv, SIB, me - 1).wait_send()

    near = z < NEAR

    @pl.when(near)
    def _():
        arrived(ent_rcv, ENT)

    def relay():
        return push_to(ent_rcv.at[core], ent_rcv.at[core], RLY, sibling)

    @pl.when(jnp.logical_not(near))
    def _():
        arrived(ent_rcv.at[core], ENT)
        relay().start()
        arrived(ent_rcv.at[1 - core], RLY)

    for b in range(BLOCKS):
        cols = slice(b * SPAN, (b + 1) * SPAN)
        for c, acc, out in ((0, y_acc, y_out), (1, r_acc, r_out)):
            entering = ent_rcv[c, b]
            both = jnp.concatenate([entering, entering], axis=0)
            total = acc[:, cols] + jnp.dot(spr[2 * core + c], both, preferred_element_type=F32)
            out[:, cols] = total.astype(BF16)

    arrived(sco_rcv, SCO)
    turned = pltpu.roll(sco_rcv[...], lax.rem(SPAN - 16 * own_part, SPAN), 1)
    s_out[...] = jnp.transpose(turned)[:OWN, :]

    @pl.when(z >= NEAR)
    def _():
        relay().wait_send()

    @pl.when(jnp.logical_and(scans, first))
    def _():
        for k in range(8):
            sent(sco_send, sco_rcv, SCO, 8 * block + k)


def last_products(
    y_ref, r_ref, go_ref, v_ref, k_ref, score_ref, gq_out, gk_out, gv_out, score_out, gq, gk, gv, score, sem
):
    score[...] = score_ref[...]
    copies = [pltpu.make_async_copy(score, score_out, sem.at[0])]
    copies[0].start()
    rows = 32
    for n in range(SPAN // rows):
        part = pl.ds(n * rows, rows)
        y = y_ref[part, :].astype(F32)
        r = r_ref[part, :].astype(F32)
        for c, (mine, gate, left, out) in enumerate(
            ((gq, go_ref, y, gq_out), (gk, v_ref, r, gk_out), (gv, k_ref, r, gv_out))
        ):
            mine[part, :] = (left * gate[part, :].astype(F32)).astype(BF16)
            copy = pltpu.make_async_copy(mine.at[part], out.at[part], sem.at[1 + 3 * n + c])
            copy.start()
            copies.append(copy)
    for copy in copies:
        copy.wait()


def body(query_gate, key_gate, value_input, grad_out, residues, decay):
    toeplitz, moments, spread = (jnp.asarray(t) for t in tables())
    tokens, channels = query_gate.shape
    vm = pltpu.VMEM
    gate = vm((tokens, channels), BF16)
    scratch = [
        gate, gate, gate, gate, vm((OWN, MODES), F32), vm((OWN, MODES), F32),
        vm(toeplitz.shape, BF16), vm(moments.shape, BF16), vm(spread.shape, BF16),
        vm((PAIR, channels), BF16), vm((PAIR, channels), BF16),
        vm((2, NODES * SPAN, channels), F32), vm((NODES, channels), F32),
        vm((tokens, channels), F32), vm((tokens, channels), F32),
        vm((NODES, channels), F32), vm((NODES, channels), F32), vm((NODES, channels // 2), F32),
        vm((BLOCKS, NODES, SPAN), BF16), vm((BLOCKS // 2, NODES, SPAN), BF16), vm((4, SPAN), F32),
        vm((CHUNKS, NODES, SPAN), BF16), vm((CHUNKS, NODES, SPAN), BF16), vm((8, 4, SPAN), F32),
        vm((BLOCKS, NODES, SPAN), BF16), vm((2, BLOCKS, NODES, SPAN), BF16), vm((MODES, SPAN), F32),
        vm((CHUNKS, MODES, SPAN), F32),
        vm((NODES, MODES, SPAN), F32), vm((MODES, NODES, SPAN), F32), vm((CHUNKS, MODES, SPAN), F32),
        vm((CHUNKS, MODES, SPAN), F32), vm((CHUNKS, NODES, SPAN), BF16), vm((NODES, SPAN), BF16),
        vm((MODES, SPAN), F32), vm((2, MODES, SPAN), F32),
        pltpu.SemaphoreType.DMA((9,)), pltpu.SemaphoreType.DMA((11,)), pltpu.SemaphoreType.DMA((11,)),
    ]
    hbm = pl.BlockSpec(memory_space=pltpu.HBM)
    vmem = pl.BlockSpec(memory_space=pltpu.VMEM)
    output, backward, score = pl.pallas_call(
        kernel,
        out_shape=(
            jax.ShapeDtypeStruct((tokens, channels), BF16),
            jax.ShapeDtypeStruct((tokens, channels), BF16),
            jax.ShapeDtypeStruct((OWN, MODES), F32),
        ),
        in_specs=[hbm] * 9,
        out_specs=(vmem, vmem, vmem),
        scratch_shapes=scratch,
        compiler_params=pltpu.CompilerParams(
            collective_id=0, has_side_effects=True, vmem_limit_bytes=48 * 2**20
        ),
        cost_estimate=pl.CostEstimate(flops=2**31, bytes_accessed=2**22, transcendentals=0),
        name="chunk_convolution",
    )(*(pltpu.with_memory_space_constraint(a, pltpu.HBM) for a in (
        query_gate, key_gate, value_input, grad_out, residues, decay, toeplitz, moments, spread)))
    wide = jax.ShapeDtypeStruct((tokens, channels), BF16)
    return pl.pallas_call(
        last_products,
        out_shape=(wide, wide, wide, jax.ShapeDtypeStruct((OWN, MODES), F32)),
        in_specs=[vmem] * 6,
        out_specs=(pl.BlockSpec(memory_space=pl.ANY),) * 4,
        scratch_shapes=[gate, gate, gate, vm((OWN, MODES), F32), pltpu.SemaphoreType.DMA((13,))],
        compiler_params=pltpu.CompilerParams(vmem_limit_bytes=8 * 2**20),
        name="last_products",
    )(output, backward, grad_out, value_input, key_gate, score)


def solution(mesh):
    gate = P("seq", "chan")
    rows = P(("chan", "seq"), None)
    return jax.shard_map(
        body,
        mesh=mesh,
        in_specs=(gate, gate, gate, gate, rows, rows),
        out_specs=(gate, gate, gate, rows),
        check_vma=False,
    )
```
